512 devices in a mesh: lat: 16 (over z, core), lon: 8 (over y), hid: 4 (over x).
Axes of the slice: x: 4, y: 8, z: 8, core: 2. Of those that a mesh axis runs over, the one named last changes fastest.
Arguments:
- grid_latent: float32 [128, 1024, 512], P('lat', 'lon'), may hold values from -6 to 6
- mesh_latent: float32 [16, 8, 512, 512], P('lat', 'lon'), may hold values from -6 to 6
- grid_edge_feats: float32 [16, 8, 4, 1024], P('lat', 'lon'), may hold values from -6 to 6
- grid_senders: int32 [16, 8, 1024], P('lat', 'lon'), may hold values from 0 to 131071, as said below
- grid_receivers: int32 [16, 8, 1024], P('lat', 'lon'), may hold values from -1 to 65535, as said below
- mesh_edge_feats: float32 [16, 8, 4, 512], P('lat', 'lon'), may hold values from -6 to 6
- mesh_senders: int32 [16, 8, 512], P('lat', 'lon'), may hold values from 0 to 65535, as said below
- mesh_receivers: int32 [16, 8, 512], P('lat', 'lon'), may hold values from -1 to 65535, as said below
- edge_weight: float32 [2, 4, 512], P(None, None, 'hid'), may hold values from -1.75 to 1.75
- sender_weight: float32 [2, 512, 512], P(None, None, 'hid'), may hold values from -0.15625 to 0.15625
- receiver_weight: float32 [2, 512, 512], P(None, None, 'hid'), may hold values from -0.15625 to 0.15625
- first_bias: float32 [2, 512], P(None, 'hid'), may hold values from -1 to 1
- out_weight: float32 [2, 512, 512], P(None, 'hid'), may hold values from -4 to 4
- out_bias: float32 [2, 512], replicated, may hold values from -3 to 3
- norm_gain: float32 [2, 512], replicated, may hold values from 0.5 to 1.5
- norm_shift: float32 [2, 512], replicated, may hold values from -3 to 3
Outputs:
- mesh_out: float32 [16, 8, 512, 512], P('lat', 'lon', None, 'hid')
The draws below stay inside these ranges and needn't reach their ends.
Inputs may be any that keep to these rules, and one draw needn't show every extreme that they name: `grid_senders`: A live slot of patch (a, b) sends from a grid cell of block (a, b) or within 2 cells outside it in latitude (never past the first or last row) and in longitude (wrapping round); a padding slot names the first cell of its own block. `grid_receivers`: in each patch's block of 1024 slots the live slots come first and their receivers are nodes of that patch in non-decreasing order; -1 marks padding; in every draw some patch has all 1024 slots live. `mesh_senders`: A live slot of patch (a, b) sends from a node of patch (a + p, b + q), p and q in -1, 0, 1, with latitude never leaving the range and longitude wrapping round; a padding slot names a node of its own patch. `mesh_receivers`: in each patch's block of 512 slots the live slots come first and their receivers are nodes of that patch in non-decreasing order; -1 marks padding; in every draw some patch has all 512 slots live.
All inputs are finite; a program needn't handle non-finite values.
Results may differ from the reference program's by a relative error of at most 0.0003.
Values sent between devices are 32-bit elements; how exact they have to be, the bound alone decides.
A program may use at most 64 MiB of HBM per device.

```python
import math
import jax
import jax.numpy as jnp
from jax import lax

C = 512
H = 512
EF = 4
RIM = 2
GLAT = 8
GLON = 128
M_DEV = 512
E2_DEV = 512
E1_DEV = 1024
PLAT = 16
PLON = 8
NLAT = 128
NLON = 1024


def patch_frame(slot_total):
    patch_row = jnp.arange(PLAT, dtype=jnp.int32)[:, None, None]
    patch_col = jnp.arange(PLON, dtype=jnp.int32)[None, :, None]
    slot_index = jnp.arange(slot_total, dtype=jnp.int32)[None, None, :]
    return (patch_row, patch_col, slot_index)


def live_slots(key_one, patch_row, slot_index, slot_total):
    polar_row = (patch_row == 0) | (patch_row == PLAT - 1)
    drawn_live = jax.random.randint(key_one, (PLAT, PLON, 1), slot_total // 2, slot_total + 1)
    live_count = jnp.where(polar_row, slot_total, drawn_live)
    return slot_index < live_count


def step_offsets(key_one, slot_shape):
    picked = jax.random.randint(key_one, slot_shape, 0, 6)
    return (picked == 5).astype(jnp.int32) - (picked == 0).astype(jnp.int32)


def receiver_ids(key_one, active, patch_row, patch_col, slot_shape):
    local_node = jax.random.randint(key_one, slot_shape, 0, M_DEV)
    local_node = jnp.sort(jnp.where(active, local_node, M_DEV), axis=-1)
    patch_number = patch_row * PLON + patch_col
    return jnp.where(active, patch_number * M_DEV + local_node, -1).astype(jnp.int32)


def grid_links(key):
    key_list = jax.random.split(jax.random.fold_in(key, 101), 8)
    slot_shape = (PLAT, PLON, E1_DEV)
    patch_row, patch_col, slot_index = patch_frame(E1_DEV)
    active = live_slots(key_list[0], patch_row, slot_index, E1_DEV)
    lat_step = step_offsets(key_list[1], slot_shape)
    lat_step = jnp.where((patch_row + lat_step < 0) | (patch_row + lat_step >= PLAT), 0, lat_step)
    lon_step = step_offsets(key_list[2], slot_shape)
    inner_row = jax.random.randint(key_list[3], slot_shape, 0, GLAT)
    inner_col = jax.random.randint(key_list[4], slot_shape, 0, GLON)
    rim_row = jax.random.randint(key_list[5], slot_shape, 0, RIM)
    rim_col = jax.random.randint(key_list[6], slot_shape, 0, RIM)
    cell_row = jnp.where(lat_step == 0, patch_row * GLAT + inner_row, jnp.where(lat_step < 0, patch_row * GLAT - 1 - rim_row, (patch_row + 1) * GLAT + rim_row))
    cell_col = jnp.where(lon_step == 0, patch_col * GLON + inner_col, jnp.where(lon_step < 0, patch_col * GLON - 1 - rim_col, (patch_col + 1) * GLON + rim_col)) % NLON
    senders = jnp.where(active, cell_row * NLON + cell_col, patch_row * GLAT * NLON + patch_col * GLON).astype(jnp.int32)
    receivers = receiver_ids(key_list[7], active, patch_row, patch_col, slot_shape)
    return (senders, receivers)


def mesh_links(key):
    key_list = jax.random.split(jax.random.fold_in(key, 202), 5)
    slot_shape = (PLAT, PLON, E2_DEV)
    patch_row, patch_col, slot_index = patch_frame(E2_DEV)
    active = live_slots(key_list[0], patch_row, slot_index, E2_DEV)
    lat_step = step_offsets(key_list[1], slot_shape)
    lat_step = jnp.where((patch_row + lat_step < 0) | (patch_row + lat_step >= PLAT), 0, lat_step)
    lon_step = step_offsets(key_list[2], slot_shape)
    source_row = patch_row + jnp.where(active, lat_step, 0)
    source_col = (patch_col + jnp.where(active, lon_step, 0)) % PLON
    source_node = jax.random.randint(key_list[3], slot_shape, 0, M_DEV)
    senders = ((source_row * PLON + source_col) * M_DEV + source_node).astype(jnp.int32)
    receivers = receiver_ids(key_list[4], active, patch_row, patch_col, slot_shape)
    return (senders, receivers)


def draw_grid_senders(key, part):
    return grid_links(key)[0]


def draw_grid_receivers(key, part):
    return grid_links(key)[1]


def draw_mesh_senders(key, part):
    return mesh_links(key)[0]


def draw_mesh_receivers(key, part):
    return mesh_links(key)[1]


def draw_out_weight(key, part):
    key_list = jax.random.split(jax.random.fold_in(key, 303), 3)
    spread = math.log(10.0) / 2.0
    row_scale = jnp.exp(jax.random.uniform(key_list[0], (2, H, 1), minval=-spread, maxval=spread))
    col_scale = jnp.exp(jax.random.uniform(key_list[1], (2, 1, C), minval=-spread, maxval=spread))
    values = jnp.clip(jax.random.normal(key_list[2], (2, H, C)), -2.5, 2.5) * row_scale * col_scale
    return (values / math.sqrt(H)).astype(jnp.float32)


def shard_levels(rng, dims, cuts, low, high):
    factor_of = 1.0
    for axis_at, blocks in cuts:
        heights = jax.random.uniform(jax.random.fold_in(jax.random.fold_in(rng, 6), axis_at), (blocks,), jnp.float32, low / len(cuts), high / len(cuts))
        factor_of = factor_of * jnp.repeat(jnp.exp(heights), dims[axis_at] // blocks).reshape((-1,) + (1,) * (len(dims) - 1 - axis_at))
    return factor_of


def noise(rng, dims, deviation, limit, cuts=(), held_as=jnp.bfloat16):
    values = jax.random.normal(rng, dims, jnp.float32) * deviation
    if len(cuts) > 0:
        values = shard_levels(rng, dims, cuts, -0.22, 0.18) * values
    return jnp.clip(values, min=-limit, max=limit).astype(held_as)


def setup_inputs(seed: int = 0) -> dict:
    seeds = jax.random.split(jax.random.key(seed), 17)
    return {
        "grid_latent": noise(seeds[0], (NLAT, NLON, C), 1.0, 6.0, ((0, 16), (1, 8)), jnp.float32),
        "mesh_latent": noise(seeds[1], (PLAT, PLON, M_DEV, C), 1.0, 6.0, ((0, 16), (1, 8)), jnp.float32),
        "grid_edge_feats": noise(seeds[2], (PLAT, PLON, EF, E1_DEV), 1.0, 6.0, ((0, 16), (1, 8)), jnp.float32),
        "grid_senders": draw_grid_senders(jax.random.fold_in(seeds[16], 71), 0),
        "grid_receivers": draw_grid_receivers(jax.random.fold_in(seeds[16], 71), 0),
        "mesh_edge_feats": noise(seeds[5], (PLAT, PLON, EF, E2_DEV), 1.0, 6.0, ((0, 16), (1, 8)), jnp.float32),
        "mesh_senders": draw_mesh_senders(jax.random.fold_in(seeds[16], 71), 0),
        "mesh_receivers": draw_mesh_receivers(jax.random.fold_in(seeds[16], 71), 0),
        "edge_weight": noise(seeds[8], (2, EF, H), (3 * EF) ** -0.5, 1.75, ((2, 4),), jnp.float32),
        "sender_weight": noise(seeds[9], (2, C, H), (3 * C) ** -0.5, 0.15625, ((2, 4),), jnp.float32),
        "receiver_weight": noise(seeds[10], (2, C, H), (3 * C) ** -0.5, 0.15625, ((2, 4),), jnp.float32),
        "first_bias": jnp.clip(jax.random.uniform(seeds[11], (2, H), jnp.float32, -1.0, 1.0) * shard_levels(seeds[11], (2, H), ((1, 4),), -0.4, 0.0), -1.0, 1.0),
        "out_weight": draw_out_weight(jax.random.fold_in(seeds[16], 71), 0),
        "out_bias": noise(seeds[13], (2, C), 0.5, 3.0, (), jnp.float32),
        "norm_gain": jnp.clip(jax.random.uniform(seeds[14], (2, C), jnp.float32, 0.5, 1.5), 0.5, 1.5),
        "norm_shift": noise(seeds[15], (2, C), 0.5, 3.0, (), jnp.float32),
    }


HIGHEST = lax.Precision.HIGHEST
epsilon = 1e-05

def matmul(left, right):
    return jnp.dot(left, right, precision=HIGHEST, preferred_element_type=jnp.float32)

def contract_first(left, right):
    return lax.dot_general(left, right, (((0,), (0,)), ((), ())), precision=HIGHEST, preferred_element_type=jnp.float32)

def layer_norm(values, gain_row, shift_row):
    center = lax.optimization_barrier(jnp.mean(values, axis=1, keepdims=True))
    centred = values - center
    spread = lax.optimization_barrier(jnp.mean(centred * centred, axis=1, keepdims=True))
    return centred * lax.rsqrt(spread + epsilon) * gain_row + shift_row

def edge_section(section_index, send_table, recv_table, feats, senders, receivers, edge_weight, sender_weight, receiver_weight, first_bias, out_weight, out_bias, norm_gain, norm_shift):
    send_terms = matmul(send_table, sender_weight[section_index])
    recv_terms = matmul(recv_table, receiver_weight[section_index])
    patch_total = PLAT * PLON
    slot_count = senders.shape[-1]
    block_feats = feats.reshape(patch_total, feats.shape[2], slot_count)
    block_send = senders.reshape(patch_total, slot_count)
    block_recv = receivers.reshape(patch_total, slot_count)

    def one_patch(bundle):
        place, feat_block, send_ids, recv_ids = bundle
        local_node = jnp.clip(recv_ids - place * M_DEV, 0, M_DEV - 1).astype(jnp.int32)
        global_node = (place * M_DEV + local_node).astype(jnp.int32)
        active = recv_ids >= 0
        hidden = jax.nn.silu(send_terms[send_ids] + recv_terms[global_node] + contract_first(feat_block, edge_weight[section_index]) + first_bias[section_index])
        message = matmul(hidden, out_weight[section_index]) + out_bias[section_index]
        normed = layer_norm(message, norm_gain[section_index], norm_shift[section_index])
        normed = jnp.where(active[:, None], normed, jnp.zeros_like(normed))
        return jax.ops.segment_sum(normed, local_node, num_segments=M_DEV)
    totals = lax.map(one_patch, (jnp.arange(patch_total, dtype=jnp.int32), block_feats, block_send, block_recv))
    return totals.reshape(patch_total * M_DEV, -1)

def reference(grid_latent, mesh_latent, grid_edge_feats, grid_senders, grid_receivers, mesh_edge_feats, mesh_senders, mesh_receivers, edge_weight, sender_weight, receiver_weight, first_bias, out_weight, out_bias, norm_gain, norm_shift):
    weights = (edge_weight, sender_weight, receiver_weight, first_bias, out_weight, out_bias, norm_gain, norm_shift)
    grid_table = grid_latent.reshape(-1, C)
    mesh_table = mesh_latent.reshape(-1, C)
    mesh_mid = mesh_table + edge_section(0, grid_table, mesh_table, grid_edge_feats, grid_senders, grid_receivers, *weights)
    mesh_out = mesh_mid + edge_section(1, mesh_mid, mesh_mid, mesh_edge_feats, mesh_senders, mesh_receivers, *weights)
    return mesh_out.reshape(PLAT, PLON, M_DEV, C)
```

```python
import jax
import jax.numpy as jnp
from jax import lax
from jax.experimental import pallas as pl
from jax.experimental.pallas import tpu as pltpu
from jax.sharding import PartitionSpec as P

MESH = pl.DeviceIdType.MESH
F32 = jnp.float32
BF16 = jnp.bfloat16
EPS = 1e-05
NLAT, NLON, NHID = 16, 8, 4
C = 512
NODES = 512
GROWS, GCOLS = 8, 128
E1, E2 = 1024, 512
Q2 = E2 // NHID
TABLE = 12 * GCOLS + 96
LEFT = 12 * GCOLS
RIGHT = LEFT + 48
RW, SW, OW = 0, 1, 2


def split(x):
    hi = x.astype(BF16)
    return hi, (x - hi.astype(F32)).astype(BF16)


def dot(a, b):
    return jnp.dot(a, b, preferred_element_type=F32)


def thrice(x):
    hi, lo = split(x)
    return jnp.concatenate([hi, hi, lo], axis=1)


def silu(t):
    return t / (1.0 + jnp.exp(-t))


def layer_norm(m, gain, shift):
    center = jnp.mean(m, axis=1, keepdims=True)
    d = m - center
    spread = jnp.mean(d * d, axis=1, keepdims=True)
    return d * lax.rsqrt(spread + EPS) * gain + shift


def kernel(
    gl, ml, gef, gs, gr, mef, ms, mr, ew, sw, rw, fb, ow, ob, ng, ns,
    out,
    table, mid, xs, idx_v, idx_s, wcol, wout, w3, r2, sel, agg, nrm, ewb, fbb, epack, wpack,
    req, gbuf, rlat, ry, n1, rm, midb,
    load_sem, wx_s, wx_r, wy_s, wy_r, wc_s, wc_r, hx_s, hx_r, q_s, q_r, gl_s, gl_r, gy_s, gy_r,
    a_s, a_r,
):
    a = lax.axis_index("lat")
    b = lax.axis_index("lon")
    h = lax.axis_index("hid")
    core = lax.rem(a, 2)
    ypar = lax.rem(b, 2)
    sib = a + 1 - 2 * core
    zlat = lax.rem(a + NLAT - 1 + 2 * core, NLAT)
    lats = (zlat, sib, a)
    lons = (lax.rem(b + NLON - 1, NLON), b, lax.rem(b + 1, NLON))
    peers = [lax.rem(h + d, NHID) for d in (1, 2, 3)]
    patch = a * NLON + b

    def dev(group, q):
        return (lats[group], lons[q + 1], h)

    around = [(g, q) for g in range(3) for q in (-1, 0, 1) if not (g == 2 and q == 0)]

    barrier = pltpu.get_barrier_semaphore()
    for p in peers:
        pl.semaphore_signal(barrier, inc=1, device_id=(a, b, p), device_id_type=MESH)
    for g, q in around:
        pl.semaphore_signal(barrier, inc=1, device_id=dev(g, q), device_id_type=MESH)

    sent = []

    def send(src, dst, ssem, rsem, device):
        copy = pltpu.make_async_remote_copy(
            src_ref=src, dst_ref=dst, send_sem=ssem, recv_sem=rsem,
            device_id=device, device_id_type=MESH,
        )
        copy.start()
        sent.append(copy)

    def arrived(dst, rsem, device):
        pltpu.make_async_remote_copy(
            src_ref=dst, dst_ref=dst, send_sem=rsem, recv_sem=rsem,
            device_id=device, device_id_type=MESH,
        ).wait_recv()

    own_rows = table.at[pl.ds(2 * GCOLS, GROWS * GCOLS)]
    load_grid = pltpu.make_async_copy(gl, own_rows, load_sem.at[0])
    load_mesh = pltpu.make_async_copy(ml.at[0, 0], mid, load_sem.at[1])
    load_grid.start()
    load_mesh.start()
    own_loads = []
    for s in range(2):
        for i, (src, dst) in enumerate(
            ((rw.at[s], wcol.at[s, RW, h]), (sw.at[s], wcol.at[s, SW, h]), (ow.at[s], wout.at[s, h]))
        ):
            copy = pltpu.make_async_copy(src, dst, load_sem.at[2 + s * 3 + i])
            copy.start()
            own_loads.append(copy)

    ids = gs[0]
    lrow = lax.shift_right_logical(ids, 10) - a * GROWS + 2
    lcol = (lax.bitwise_and(ids, 1023) - b * GCOLS + 2 + 1024) & 1023
    side = (lrow + 6) * 2
    where = jnp.where(
        lcol < 2,
        LEFT + side + lcol,
        jnp.where(lcol >= GCOLS + 2, RIGHT + side + lcol - (GCOLS + 2), lrow * GCOLS + lcol - 2),
    )
    idx_v[...] = jnp.clip(where, 0, TABLE - 1)
    to_smem = pltpu.make_async_copy(idx_v, idx_s, load_sem.at[8])
    to_smem.start()

    pl.semaphore_wait(barrier, 11)

    low = table.at[pl.ds(0, 2 * GCOLS)]
    high = table.at[pl.ds(10 * GCOLS, 2 * GCOLS)]
    top = gl.at[pl.ds(6 * GCOLS, 2 * GCOLS)]
    bottom = gl.at[pl.ds(0, 2 * GCOLS)]
    up = lax.rem(a + 1, NLAT)
    down = lax.rem(a + NLAT - 1, NLAT)
    send(top, low, hx_s.at[0], hx_r.at[0], (up, b, h))
    send(bottom, high, hx_s.at[1], hx_r.at[1], (down, b, h))

    def src_of(s, m):
        return (rw, sw, ow)[m].at[s]

    def dst_of(s, m, who):
        return wout.at[s, who] if m == OW else wcol.at[s, m, who]

    def size_of(m):
        return 32 if m == OW else 128

    def piece(ref, m, which):
        n = size_of(m)
        return ref.at[pl.ds(pl.multiple_of(which * n, n), n)]

    def half(ref, m, which, part):
        n = size_of(m) // 2
        return ref.at[pl.ds(pl.multiple_of(which * 2 * n + part * n, n), n)]

    mine = 2 * core + ypar
    other = 2 * core + 1 - ypar
    sib_mine = 2 * (1 - core) + ypar
    sib_other = 2 * (1 - core) + 1 - ypar

    def x_send(s, m):
        for i, p in enumerate(peers):
            send(
                piece(src_of(s, m), m, mine), piece(dst_of(s, m, h), m, mine),
                wx_s.at[s, m, i], wx_r.at[s, m, i], (a, b, p),
            )

    def x_forward(s, m):
        for i in range(3):
            owner = peers[2 - i]
            arrived(piece(dst_of(s, m, owner), m, mine), wx_r.at[s, m, i], (a, b, owner))
            for part, q in ((0, 1), (1, -1)):
                view = half(dst_of(s, m, owner), m, mine, part)
                send(view, view, wy_s.at[s, m, i, part], wy_r.at[s, m, i, part], dev(2, q))
            view = piece(dst_of(s, m, owner), m, mine)
            send(view, view, wc_s.at[s, m, i, 0], wc_r.at[s, m, i, 0], dev(1, 0))

    def y_forward(s, m):
        for i in range(3):
            owner = peers[2 - i]
            for part, q in ((0, -1), (1, 1)):
                arrived(half(dst_of(s, m, owner), m, other, part), wy_r.at[s, m, i, part], dev(2, q))
            view = piece(dst_of(s, m, owner), m, other)
            send(view, view, wc_s.at[s, m, i, 1], wc_r.at[s, m, i, 1], dev(1, 0))

    def c_wait(s, m):
        for i in range(3):
            owner = peers[2 - i]
            arrived(piece(dst_of(s, m, owner), m, sib_mine), wc_r.at[s, m, i, 0], dev(1, 0))
            arrived(piece(dst_of(s, m, owner), m, sib_other), wc_r.at[s, m, i, 1], dev(1, 0))

    def build(s, m):
        own_loads[s * 3 + m].wait()
        for k in range(NHID):
            block = wout[s, k] if m == OW else wcol[s, m, k]
            hi, lo = split(block)
            if m == OW:
                for t, v in enumerate((hi, lo, hi)):
                    w3[s, m, pl.ds(t * 512 + k * 128, 128), :] = v
            else:
                for t, v in enumerate((hi, lo, hi)):
                    w3[s, m, pl.ds(t * 512, 512), pl.ds(k * 128, 128)] = v

    x_send(0, RW)
    for i, p in enumerate(peers):
        send(ew, ewb.at[h], hx_s.at[2 + i], hx_r.at[2 + i], (a, b, p))
        send(fb, fbb.at[h], hx_s.at[5 + i], hx_r.at[5 + i], (a, b, p))
    x_send(0, SW)
    x_send(0, OW)
    lanes = pl.ds(pl.multiple_of(h * Q2, Q2), Q2)
    for i, (g, q) in enumerate(around):
        send(ms.at[0, :, lanes], req.at[g, 1 - q], q_s.at[g, q + 1], q_r.at[g, 1 - q], dev(g, q))
    req[2, 1] = ms[0, :, lanes]
    ewb[h] = ew[...]
    fbb[h] = fb[...]

    load_grid.wait()
    for r in range(GROWS):
        base = (2 + r) * GCOLS
        wpack[pl.ds(2 * r, 2), :] = table[pl.ds(base, 2), :]
        epack[pl.ds(2 * r, 2), :] = table[pl.ds(base + GCOLS - 2, 2), :]
    for j, g in enumerate((0, 1, 2)):
        if g == 0:
            seg_at_target = 32 * (1 - core)
        elif g == 1:
            seg_at_target = 32 * core
        else:
            seg_at_target = 16
        for side_i, (pack, base, q) in enumerate(((epack, LEFT, 1), (wpack, RIGHT, -1))):
            send(
                pack, table.at[pl.ds(pl.multiple_of(base + seg_at_target, 16), 16)],
                hx_s.at[8 + 2 * j + side_i], hx_r.at[8 + 2 * j + side_i], dev(g, q),
            )

    x_forward(0, RW)

    local = (gr[0] - patch * NODES).astype(F32)
    node_rows = lax.broadcasted_iota(jnp.int32, (NODES, 128), 0).astype(F32)
    node_lanes = lax.broadcasted_iota(jnp.int32, (128, NODES), 1).astype(F32)

    def agg_block(row):
        return jnp.where(node_rows == row, 1.0, 0.0).astype(BF16)

    def sel_block(row):
        col = jnp.transpose(jnp.broadcast_to(row, (128, 128)))
        return jnp.where(node_lanes == jnp.concatenate([col] * 4, axis=1), 1.0, 0.0).astype(BF16)

    for j in range(E1 // 128):
        row = local[:, j * 128 : (j + 1) * 128]
        agg[:, pl.ds(j * 128, 128)] = agg_block(row)
        sel[pl.ds(j * 128, 128), :] = sel_block(row)

    x_forward(0, SW)
    y_forward(0, RW)
    x_forward(0, OW)
    y_forward(0, SW)
    for m in (RW, SW, OW):
        x_send(1, m)

    for i in range(3):
        arrived(ewb.at[peers[2 - i]], hx_r.at[2 + i], (a, b, peers[2 - i]))
        arrived(fbb.at[peers[2 - i]], hx_r.at[5 + i], (a, b, peers[2 - i]))

    def edge_weights(s):
        w = jnp.concatenate([ewb[k, s] for k in range(NHID)], axis=1)
        bias = jnp.concatenate([fbb[k, pl.ds(s, 1)] for k in range(NHID)], axis=1)
        wh = w.astype(BF16).astype(F32)
        bh = bias.astype(BF16).astype(F32)
        bl = (bias - bh).astype(BF16).astype(F32)
        bll = bias - bh - bl
        rows = [wh, w - wh, wh, bh, bl, bll, jnp.zeros_like(bll)]
        return jnp.concatenate(rows, axis=0).astype(BF16)

    def edge_feats(f):
        fh = f.astype(BF16).astype(F32)
        rows = [fh, fh, f - fh, jnp.ones_like(f)]
        return jnp.transpose(jnp.concatenate(rows, axis=0)).astype(BF16)

    ew0 = edge_weights(0)

    load_mesh.wait()
    c_wait(0, RW)
    build(0, RW)
    y_forward(0, OW)
    terms = dot(thrice(mid[...]), w3[0, RW])
    hi, lo = split(terms)
    r2[pl.ds(0, 512), :] = hi
    r2[pl.ds(512, 512), :] = lo

    c_wait(0, SW)
    build(0, SW)
    x_forward(1, RW)
    c_wait(0, OW)
    build(0, OW)
    x_forward(1, SW)

    to_smem.wait()
    arrived(low, hx_r.at[0], (down, b, h))
    arrived(high, hx_r.at[1], (up, b, h))
    for j, g in enumerate((0, 1, 2)):
        if g == 0:
            seg = 32 * core
        elif g == 1:
            seg = 32 * (1 - core)
        else:
            seg = 16
        for side_i, (base, q) in enumerate(((LEFT, -1), (RIGHT, 1))):
            arrived(
                table.at[pl.ds(pl.multiple_of(base + seg, 16), 16)],
                hx_r.at[8 + 2 * j + side_i], dev(g, q),
            )

    def take_rows(i, carry):
        for k in range(8):
            e = i * 8 + k
            xs[pl.ds(e, 1), :] = table[pl.ds(idx_s[0, e], 1), :]
        return carry

    lax.fori_loop(0, E1 // 8, take_rows, 0)
    x_forward(1, OW)
    y_forward(1, RW)

    STEP = 256
    for j in range(E1 // STEP):
        rows = pl.ds(j * STEP, STEP)
        one = sel[rows, :]
        pre = dot(thrice(xs[rows, :]), w3[0, SW])
        pre += dot(jnp.concatenate([one, one], axis=1), r2[...])
        pre += dot(edge_feats(gef[0, 0, :, j * STEP : (j + 1) * STEP]), ew0)
        hidden = silu(pre)
        message = dot(thrice(hidden), w3[0, OW]) + ob[pl.ds(0, 1), :]
        hi, lo = split(layer_norm(message, ng[pl.ds(0, 1), :], ns[pl.ds(0, 1), :]))
        nrm[rows, :] = hi
        nrm[pl.ds(E1 + j * STEP, STEP), :] = lo
        if j == 0:
            y_forward(1, SW)
        if j == 1:
            y_forward(1, OW)
        if j == 2:
            c_wait(1, SW)
            build(1, SW)

    both = agg[...]
    mid[...] += dot(jnp.concatenate([both, both], axis=1), nrm[...])
    mid3 = thrice(mid[...])
    hi, lo = split(dot(mid3, w3[1, SW]))
    r2[pl.ds(0, 512), :] = hi
    r2[pl.ds(512, 512), :] = lo

    for i, (g, q) in enumerate(around):
        arrived(req.at[g, q + 1], q_r.at[g, q + 1], dev(g, q))

    def contributions(g):
        picks = [sel_block((req[g, t] - patch * NODES).astype(F32)) for t in range(3)]
        picks = jnp.concatenate(picks, axis=0)
        found = dot(jnp.concatenate([picks, picks], axis=1), r2[...])
        for t in range(3):
            gbuf[g, t] = found[t * 128 : (t + 1) * 128]

    for g in range(2):
        contributions(g)
        for t in (0, 2, 1):
            send(gbuf.at[g, t], rlat.at[g, t], gl_s.at[g, t], gl_r.at[g, t], dev(g, 0))
    contributions(2)

    for m in (RW, OW):
        c_wait(1, m)
        build(1, m)
    local2 = (mr[0] - patch * NODES).astype(F32)
    for j in range(E2 // 128):
        agg[:, pl.ds(j * 128, 128)] = agg_block(local2[:, j * 128 : (j + 1) * 128])
    for k in range(NHID):
        midb[k] = mid[:, k * 128 : (k + 1) * 128]
    mine_recv = (mr[0, :, lanes] - patch * NODES).astype(F32)
    one = sel_block(mine_recv)
    mh, mlo = split(mid[...])
    picked = dot(one, mh) + dot(one, mlo)
    pre = dot(thrice(picked), w3[1, RW]) + dot(edge_feats(mef[0, 0, :, lanes]), edge_weights(1))

    for t, q in ((0, -1), (2, 1), (1, 0)):
        for g in (1, 0):
            arrived(rlat.at[g, t], gl_r.at[g, t], dev(g, 0))
        gbuf[2, t] = gbuf[2, t] + rlat[0, t] + rlat[1, t]
        if q != 0:
            send(gbuf.at[2, t], ry.at[1 if q < 0 else 0], gy_s.at[t], gy_r.at[1 if q < 0 else 0], dev(2, q))
    pre += gbuf[2, 1]
    arrived(ry.at[1], gy_r.at[1], dev(2, 1))
    arrived(ry.at[0], gy_r.at[0], dev(2, -1))
    pre += ry[0] + ry[1]
    message = dot(thrice(silu(pre)), w3[1, OW]) + ob[pl.ds(1, 1), :]
    normed = layer_norm(message, ng[pl.ds(1, 1), :], ns[pl.ds(1, 1), :])
    for k in range(NHID):
        n1[k] = normed[:, k * 128 : (k + 1) * 128]
    for i, p in enumerate(peers):
        send(n1.at[p], rm.at[h], a_s.at[i], a_r.at[i], (a, b, p))
    rm[h] = n1[h]
    for i in range(3):
        owner = peers[2 - i]
        arrived(rm.at[owner], a_r.at[i], (a, b, owner))
    hi, lo = split(rm[...].reshape(E2, 128))
    one = agg[:, pl.ds(0, E2)]
    out[0, 0] = midb[h] + dot(one, hi) + dot(one, lo)
    for copy in sent:
        copy.wait_send()


def per_device(gl, *rest):
    dma = pltpu.SemaphoreType.DMA
    vmem = pl.BlockSpec(memory_space=pltpu.VMEM)
    hbm = pl.BlockSpec(memory_space=pl.ANY)
    specs = [hbm, hbm, vmem, vmem, vmem, vmem, vmem, vmem, vmem, hbm, hbm, vmem, hbm, vmem, vmem, vmem]
    scratch = [
        pltpu.VMEM((TABLE, C), F32),
        pltpu.VMEM((NODES, C), F32),
        pltpu.VMEM((E1, C), F32),
        pltpu.VMEM((1, E1), jnp.int32),
        pltpu.SMEM((1, E1), jnp.int32),
        pltpu.VMEM((2, 2, NHID, 512, 128), F32),
        pltpu.VMEM((2, NHID, 128, 512), F32),
        pltpu.VMEM((2, 3, 1536, 512), BF16),
        pltpu.VMEM((1024, 512), BF16),
        pltpu.VMEM((E1, NODES), BF16),
        pltpu.VMEM((NODES, E1), BF16),
        pltpu.VMEM((2 * E1, C), BF16),
        pltpu.VMEM((NHID, 2, 4, 128), F32),
        pltpu.VMEM((NHID, 2, 128), F32),
        pltpu.VMEM((16, C), F32),
        pltpu.VMEM((16, C), F32),
        pltpu.VMEM((3, 3, 1, 128), jnp.int32),
        pltpu.VMEM((3, 3, 128, C), F32),
        pltpu.VMEM((2, 3, 128, C), F32),
        pltpu.VMEM((2, 128, C), F32),
        pltpu.VMEM((NHID, 128, 128), F32),
        pltpu.VMEM((NHID, 128, 128), F32),
        pltpu.VMEM((NHID, NODES, 128), F32),
        dma((9,)),
        dma((2, 3, 3)), dma((2, 3, 3)),
        dma((2, 3, 3, 2)), dma((2, 3, 3, 2)),
        dma((2, 3, 3, 2)), dma((2, 3, 3, 2)),
        dma((14,)), dma((14,)),
        dma((3, 3)), dma((3, 3)),
        dma((2, 3)), dma((2, 3)),
        dma((3,)), dma((2,)),
        dma((3,)), dma((3,)),
    ]
    return pl.pallas_call(
        kernel,
        out_shape=jax.ShapeDtypeStruct((1, 1, NODES, 128), F32),
        in_specs=specs,
        out_specs=vmem,
        scratch_shapes=scratch,
        compiler_params=pltpu.CompilerParams(
            collective_id=0, has_side_effects=True, vmem_limit_bytes=56 * 2**20
        ),
        cost_estimate=pl.CostEstimate(flops=10**10, bytes_accessed=10**7, transcendentals=10**6),
    )(gl.reshape(GROWS * GCOLS, C), *rest)


def solution(mesh):
    return jax.shard_map(
        per_device,
        mesh=mesh,
        in_specs=(
            P("lat", "lon", None),
            P("lat", "lon", None, None),
            P("lat", "lon", None, None),
            P("lat", "lon", None),
            P("lat", "lon", None),
            P("lat", "lon", None, None),
            P("lat", "lon", None),
            P("lat", "lon", None),
            P(None, None, "hid"),
            P(None, None, "hid"),
            P(None, None, "hid"),
            P(None, "hid"),
            P(None, "hid", None),
            P(),
            P(),
            P(),
        ),
        out_specs=P("lat", "lon", None, "hid"),
        check_vma=False,
    )
```

```python
import jax
import jax.numpy as jnp
from jax import lax
from jax.experimental import pallas as pl
from jax.experimental.pallas import tpu as pltpu
from jax.sharding import PartitionSpec as P

MESH = pl.DeviceIdType.MESH
F32 = jnp.float32
BF16 = jnp.bfloat16
EPS = 1e-05
NLAT, NLON, NHID = 16, 8, 4
C = 512
NODES = 512
GROWS, GCOLS = 8, 128
E1, E2 = 1024, 512
Q2 = E2 // NHID
TABLE = 12 * GCOLS + 96
LEFT = 12 * GCOLS
RIGHT = LEFT + 48
RW, SW, OW = 0, 1, 2


def split(x):
    hi = x.astype(BF16)
    return hi, (x - hi.astype(F32)).astype(BF16)


def dot(a, b):
    return jnp.dot(a, b, preferred_element_type=F32)


def thrice(x):
    hi, lo = split(x)
    return jnp.concatenate([hi, hi, lo], axis=1)


def silu(t):
    return t / (1.0 + jnp.exp(-t))


def layer_norm(m, gain, shift):
    center = jnp.mean(m, axis=1, keepdims=True)
    d = m - center
    spread = jnp.mean(d * d, axis=1, keepdims=True)
    return d * lax.rsqrt(spread + EPS) * gain + shift


def kernel(
    gl, ml, gef, gs, gr, mef, ms, mr, ew, sw, rw, fb, ow, ob, ng, ns,
    out,
    table, mid, xs, idx_v, idx_s, wcol, wout, w3, r2, sel, agg, nrm, ewb, fbb, epack, wpack,
    req, gbuf, rlat, ry, rdiag, n1, rm, midb,
    load_sem, wx_s, wx_r, wy_s, wy_r, wc_s, wc_r, hx_s, hx_r, q_s, q_r, gl_s, gl_r, gy_s, gy_r,
    gd_s, gd_r, a_s, a_r,
):
    a = lax.axis_index("lat")
    b = lax.axis_index("lon")
    h = lax.axis_index("hid")
    core = lax.rem(a, 2)
    ypar = lax.rem(b, 2)
    sib = a + 1 - 2 * core
    zlat = lax.rem(a + NLAT - 1 + 2 * core, NLAT)
    lats = (zlat, sib, a)
    lons = (lax.rem(b + NLON - 1, NLON), b, lax.rem(b + 1, NLON))
    peers = [lax.rem(h + d, NHID) for d in (1, 2, 3)]
    patch = a * NLON + b

    def dev(group, q):
        return (lats[group], lons[q + 1], h)

    around = [(g, q) for g in range(3) for q in (-1, 0, 1) if not (g == 2 and q == 0)]

    barrier = pltpu.get_barrier_semaphore()
    for p in peers:
        pl.semaphore_signal(barrier, inc=1, device_id=(a, b, p), device_id_type=MESH)
    for g, q in around:
        pl.semaphore_signal(barrier, inc=1, device_id=dev(g, q), device_id_type=MESH)

    sent = []

    def send(src, dst, ssem, rsem, device):
        copy = pltpu.make_async_remote_copy(
            src_ref=src, dst_ref=dst, send_sem=ssem, recv_sem=rsem,
            device_id=device, device_id_type=MESH,
        )
        copy.start()
        sent.append(copy)

    def arrived(dst, rsem, device):
        pltpu.make_async_remote_copy(
            src_ref=dst, dst_ref=dst, send_sem=rsem, recv_sem=rsem,
            device_id=device, device_id_type=MESH,
        ).wait_recv()

    own_rows = table.at[pl.ds(2 * GCOLS, GROWS * GCOLS)]
    load_grid = pltpu.make_async_copy(gl, own_rows, load_sem.at[0])
    load_mesh = pltpu.make_async_copy(ml.at[0, 0], mid, load_sem.at[1])
    load_grid.start()
    load_mesh.start()
    own_loads = []
    for s in range(2):
        for i, (src, dst) in enumerate(
            ((rw.at[s], wcol.at[s, RW, h]), (sw.at[s], wcol.at[s, SW, h]), (ow.at[s], wout.at[s, h]))
        ):
            copy = pltpu.make_async_copy(src, dst, load_sem.at[2 + s * 3 + i])
            copy.start()
            own_loads.append(copy)

    ids = gs[0]
    lrow = lax.shift_right_logical(ids, 10) - a * GROWS + 2
    lcol = (lax.bitwise_and(ids, 1023) - b * GCOLS + 2 + 1024) & 1023
    side = (lrow + 6) * 2
    where = jnp.where(
        lcol < 2,
        LEFT + side + lcol,
        jnp.where(lcol >= GCOLS + 2, RIGHT + side + lcol - (GCOLS + 2), lrow * GCOLS + lcol - 2),
    )
    idx_v[...] = jnp.clip(where, 0, TABLE - 1)
    to_smem = pltpu.make_async_copy(idx_v, idx_s, load_sem.at[8])
    to_smem.start()

    pl.semaphore_wait(barrier, 11)

    low = table.at[pl.ds(0, 2 * GCOLS)]
    high = table.at[pl.ds(10 * GCOLS, 2 * GCOLS)]
    top = gl.at[pl.ds(6 * GCOLS, 2 * GCOLS)]
    bottom = gl.at[pl.ds(0, 2 * GCOLS)]
    up = lax.rem(a + 1, NLAT)
    down = lax.rem(a + NLAT - 1, NLAT)
    send(top, low, hx_s.at[0], hx_r.at[0], (up, b, h))
    send(bottom, high, hx_s.at[1], hx_r.at[1], (down, b, h))

    def src_of(s, m):
        return (rw, sw, ow)[m].at[s]

    def dst_of(s, m, who):
        return wout.at[s, who] if m == OW else wcol.at[s, m, who]

    def size_of(m):
        return 32 if m == OW else 128

    def piece(ref, m, which):
        n = size_of(m)
        return ref.at[pl.ds(pl.multiple_of(which * n, n), n)]

    def half(ref, m, which, part):
        n = size_of(m) // 2
        return ref.at[pl.ds(pl.multiple_of(which * 2 * n + part * n, n), n)]

    mine = 2 * core + ypar
    other = 2 * core + 1 - ypar
    sib_mine = 2 * (1 - core) + ypar
    sib_other = 2 * (1 - core) + 1 - ypar

    def x_send(s, m):
        for i, p in enumerate(peers):
            send(
                piece(src_of(s, m), m, mine), piece(dst_of(s, m, h), m, mine),
                wx_s.at[s, m, i], wx_r.at[s, m, i], (a, b, p),
            )

    def x_forward(s, m):
        for i in range(3):
            owner = peers[2 - i]
            arrived(piece(dst_of(s, m, owner), m, mine), wx_r.at[s, m, i], (a, b, owner))
            for part, q in ((0, 1), (1, -1)):
                view = half(dst_of(s, m, owner), m, mine, part)
                send(view, view, wy_s.at[s, m, i, part], wy_r.at[s, m, i, part], dev(2, q))
            view = piece(dst_of(s, m, owner), m, mine)
            send(view, view, wc_s.at[s, m, i, 0], wc_r.at[s, m, i, 0], dev(1, 0))

    def y_forward(s, m):
        for i in range(3):
            owner = peers[2 - i]
            for part, q in ((0, -1), (1, 1)):
                arrived(half(dst_of(s, m, owner), m, other, part), wy_r.at[s, m, i, part], dev(2, q))
            view = piece(dst_of(s, m, owner), m, other)
            send(view, view, wc_s.at[s, m, i, 1], wc_r.at[s, m, i, 1], dev(1, 0))

    def c_wait(s, m):
        for i in range(3):
            owner = peers[2 - i]
            arrived(piece(dst_of(s, m, owner), m, sib_mine), wc_r.at[s, m, i, 0], dev(1, 0))
            arrived(piece(dst_of(s, m, owner), m, sib_other), wc_r.at[s, m, i, 1], dev(1, 0))

    def build(s, m):
        own_loads[s * 3 + m].wait()
        for k in range(NHID):
            block = wout[s, k] if m == OW else wcol[s, m, k]
            hi, lo = split(block)
            if m == OW:
                for t, v in enumerate((hi, lo, hi)):
                    w3[s, m, pl.ds(t * 512 + k * 128, 128), :] = v
            else:
                for t, v in enumerate((hi, lo, hi)):
                    w3[s, m, pl.ds(t * 512, 512), pl.ds(k * 128, 128)] = v

    x_send(0, RW)
    for i, p in enumerate(peers):
        send(ew, ewb.at[h], hx_s.at[2 + i], hx_r.at[2 + i], (a, b, p))
        send(fb, fbb.at[h], hx_s.at[5 + i], hx_r.at[5 + i], (a, b, p))
    x_send(0, SW)
    x_send(0, OW)
    lanes = pl.ds(pl.multiple_of(h * Q2, Q2), Q2)
    for i, (g, q) in enumerate(around):
        send(ms.at[0, :, lanes], req.at[g, 1 - q], q_s.at[g, q + 1], q_r.at[g, 1 - q], dev(g, q))
    req[2, 1] = ms[0, :, lanes]
    ewb[h] = ew[...]
    fbb[h] = fb[...]

    load_grid.wait()
    for r in range(GROWS):
        base = (2 + r) * GCOLS
        wpack[pl.ds(2 * r, 2), :] = table[pl.ds(base, 2), :]
        epack[pl.ds(2 * r, 2), :] = table[pl.ds(base + GCOLS - 2, 2), :]
    for j, g in enumerate((0, 1, 2)):
        if g == 0:
            seg_at_target = 32 * (1 - core)
        elif g == 1:
            seg_at_target = 32 * core
        else:
            seg_at_target = 16
        for side_i, (pack, base, q) in enumerate(((epack, LEFT, 1), (wpack, RIGHT, -1))):
            send(
                pack, table.at[pl.ds(pl.multiple_of(base + seg_at_target, 16), 16)],
                hx_s.at[8 + 2 * j + side_i], hx_r.at[8 + 2 * j + side_i], dev(g, q),
            )

    x_forward(0, RW)
    x_send(1, SW)

    local = (gr[0] - patch * NODES).astype(F32)
    node_rows = lax.broadcasted_iota(jnp.int32, (NODES, 128), 0).astype(F32)
    node_lanes = lax.broadcasted_iota(jnp.int32, (128, NODES), 1).astype(F32)

    def agg_block(row):
        return jnp.where(node_rows == row, 1.0, 0.0).astype(BF16)

    def sel_block(row):
        col = jnp.transpose(jnp.broadcast_to(row, (128, 128)))
        return jnp.where(node_lanes == jnp.concatenate([col] * 4, axis=1), 1.0, 0.0).astype(BF16)

    for j in range(E1 // 128):
        row = local[:, j * 128 : (j + 1) * 128]
        agg[:, pl.ds(j * 128, 128)] = agg_block(row)
        sel[pl.ds(j * 128, 128), :] = sel_block(row)

    x_forward(0, SW)
    x_send(1, RW)
    y_forward(0, RW)
    x_forward(0, OW)
    x_send(1, OW)
    y_forward(0, SW)

    for i in range(3):
        arrived(ewb.at[peers[2 - i]], hx_r.at[2 + i], (a, b, peers[2 - i]))
        arrived(fbb.at[peers[2 - i]], hx_r.at[5 + i], (a, b, peers[2 - i]))

    def edge_weights(s):
        w = jnp.concatenate([ewb[k, s] for k in range(NHID)], axis=1)
        bias = jnp.concatenate([fbb[k, pl.ds(s, 1)] for k in range(NHID)], axis=1)
        wh = w.astype(BF16).astype(F32)
        bh = bias.astype(BF16).astype(F32)
        bl = (bias - bh).astype(BF16).astype(F32)
        bll = bias - bh - bl
        rows = [wh, w - wh, wh, bh, bl, bll, jnp.zeros_like(bll)]
        return jnp.concatenate(rows, axis=0).astype(BF16)

    def edge_feats(f):
        fh = f.astype(BF16).astype(F32)
        rows = [fh, fh, f - fh, jnp.ones_like(f)]
        return jnp.transpose(jnp.concatenate(rows, axis=0)).astype(BF16)

    ew0 = edge_weights(0)

    load_mesh.wait()
    c_wait(0, RW)
    build(0, RW)
    y_forward(0, OW)
    terms = dot(thrice(mid[...]), w3[0, RW])
    hi, lo = split(terms)
    r2[pl.ds(0, 512), :] = hi
    r2[pl.ds(512, 512), :] = lo

    c_wait(0, SW)
    build(0, SW)
    x_forward(1, SW)
    c_wait(0, OW)
    build(0, OW)

    to_smem.wait()
    arrived(low, hx_r.at[0], (down, b, h))
    arrived(high, hx_r.at[1], (up, b, h))
    for j, g in enumerate((0, 1, 2)):
        if g == 0:
            seg = 32 * core
        elif g == 1:
            seg = 32 * (1 - core)
        else:
            seg = 16
        for side_i, (base, q) in enumerate(((LEFT, -1), (RIGHT, 1))):
            arrived(
                table.at[pl.ds(pl.multiple_of(base + seg, 16), 16)],
                hx_r.at[8 + 2 * j + side_i], dev(g, q),
            )

    def take_rows(i, carry):
        for k in range(8):
            e = i * 8 + k
            xs[pl.ds(e, 1), :] = table[pl.ds(idx_s[0, e], 1), :]
        return carry

    lax.fori_loop(0, E1 // 8, take_rows, 0)
    STEP = 256
    for j in range(E1 // STEP):
        rows = pl.ds(j * STEP, STEP)
        one = sel[rows, :]
        pre = dot(thrice(xs[rows, :]), w3[0, SW])
        pre += dot(jnp.concatenate([one, one], axis=1), r2[...])
        pre += dot(edge_feats(gef[0, 0, :, j * STEP : (j + 1) * STEP]), ew0)
        hidden = silu(pre)
        message = dot(thrice(hidden), w3[0, OW]) + ob[pl.ds(0, 1), :]
        hi, lo = split(layer_norm(message, ng[pl.ds(0, 1), :], ns[pl.ds(0, 1), :]))
        nrm[rows, :] = hi
        nrm[pl.ds(E1 + j * STEP, STEP), :] = lo
        if j == 0:
            y_forward(1, SW)
        if j == 1:
            x_forward(1, RW)
        if j == 2:
            x_forward(1, OW)

    both = agg[...]
    mid[...] += dot(jnp.concatenate([both, both], axis=1), nrm[...])
    c_wait(1, SW)
    build(1, SW)
    mid3 = thrice(mid[...])
    hi, lo = split(dot(mid3, w3[1, SW]))
    r2[pl.ds(0, 512), :] = hi
    r2[pl.ds(512, 512), :] = lo

    for i, (g, q) in enumerate(around):
        arrived(req.at[g, q + 1], q_r.at[g, q + 1], dev(g, q))

    def contributions(g):
        picks = [sel_block((req[g, t] - patch * NODES).astype(F32)) for t in range(3)]
        picks = jnp.concatenate(picks, axis=0)
        found = dot(jnp.concatenate([picks, picks], axis=1), r2[...])
        for t in range(3):
            gbuf[g, t] = found[t * 128 : (t + 1) * 128]

    first, second = pl.ds(0, 64), pl.ds(64, 64)
    contributions(0)
    for t, q in ((0, -1), (2, 1)):
        send(gbuf.at[0, t, first], rlat.at[0, t, first], gl_s.at[0, t, 0], gl_r.at[0, t, 0], dev(0, 0))
        side_i = 1 if q < 0 else 0
        send(gbuf.at[0, t, second], rdiag.at[side_i], gd_s.at[t], gd_r.at[side_i], dev(2, q))
    send(gbuf.at[0, 1, first], rlat.at[0, 1, first], gl_s.at[0, 1, 0], gl_r.at[0, 1, 0], dev(0, 0))
    contributions(1)
    for t in (0, 2, 1):
        send(gbuf.at[1, t], rlat.at[1, t], gl_s.at[1, t, 0], gl_r.at[1, t, 0], dev(1, 0))
    contributions(2)
    for t, q in ((0, -1), (2, 1)):
        arrived(rlat.at[1, t], gl_r.at[1, t, 0], dev(1, 0))
        gbuf[2, t] = gbuf[2, t] + rlat[1, t]
        side_i = 1 if q < 0 else 0
        send(gbuf.at[2, t, second], ry.at[side_i, second], gy_s.at[t, 1], gy_r.at[side_i, 1], dev(2, q))
    arrived(rdiag.at[1], gd_r.at[1], dev(2, 1))
    arrived(rdiag.at[0], gd_r.at[0], dev(2, -1))
    gbuf[0, 1, second] = gbuf[0, 1, second] + rdiag[0] + rdiag[1]
    send(gbuf.at[0, 1, second], rlat.at[0, 1, second], gl_s.at[0, 1, 1], gl_r.at[0, 1, 1], dev(0, 0))
    for t, q in ((0, -1), (2, 1)):
        arrived(rlat.at[0, t, first], gl_r.at[0, t, 0], dev(0, 0))
        gbuf[2, t, first] = gbuf[2, t, first] + rlat[0, t, first]
        side_i = 1 if q < 0 else 0
        send(gbuf.at[2, t, first], ry.at[side_i, first], gy_s.at[t, 0], gy_r.at[side_i, 0], dev(2, q))
    y_forward(1, RW)
    y_forward(1, OW)

    for m in (RW, OW):
        c_wait(1, m)
        build(1, m)
    local2 = (mr[0] - patch * NODES).astype(F32)
    for j in range(E2 // 128):
        agg[:, pl.ds(j * 128, 128)] = agg_block(local2[:, j * 128 : (j + 1) * 128])
    for k in range(NHID):
        midb[k] = mid[:, k * 128 : (k + 1) * 128]
    mine_recv = (mr[0, :, lanes] - patch * NODES).astype(F32)
    one = sel_block(mine_recv)
    mh, mlo = split(mid[...])
    picked = dot(one, mh) + dot(one, mlo)
    pre = dot(thrice(picked), w3[1, RW]) + dot(edge_feats(mef[0, 0, :, lanes]), edge_weights(1))

    arrived(rlat.at[1, 1], gl_r.at[1, 1, 0], dev(1, 0))
    arrived(rlat.at[0, 1, first], gl_r.at[0, 1, 0], dev(0, 0))
    arrived(rlat.at[0, 1, second], gl_r.at[0, 1, 1], dev(0, 0))
    pre += gbuf[2, 1] + rlat[1, 1] + rlat[0, 1]
    for part, rows in ((1, second), (0, first)):
        arrived(ry.at[1, rows], gy_r.at[1, part], dev(2, 1))
        arrived(ry.at[0, rows], gy_r.at[0, part], dev(2, -1))
    pre += ry[0] + ry[1]
    message = dot(thrice(silu(pre)), w3[1, OW]) + ob[pl.ds(1, 1), :]
    normed = layer_norm(message, ng[pl.ds(1, 1), :], ns[pl.ds(1, 1), :])
    for k in range(NHID):
        n1[k] = normed[:, k * 128 : (k + 1) * 128]
    for i, p in enumerate(peers):
        send(n1.at[p], rm.at[h], a_s.at[i], a_r.at[i], (a, b, p))
    rm[h] = n1[h]
    for i in range(3):
        owner = peers[2 - i]
        arrived(rm.at[owner], a_r.at[i], (a, b, owner))
    hi, lo = split(rm[...].reshape(E2, 128))
    one = agg[:, pl.ds(0, E2)]
    out[0, 0] = midb[h] + dot(one, hi) + dot(one, lo)
    for copy in sent:
        copy.wait_send()


def per_device(gl, *rest):
    dma = pltpu.SemaphoreType.DMA
    vmem = pl.BlockSpec(memory_space=pltpu.VMEM)
    hbm = pl.BlockSpec(memory_space=pl.ANY)
    specs = [hbm, hbm, vmem, vmem, vmem, vmem, vmem, vmem, vmem, hbm, hbm, vmem, hbm, vmem, vmem, vmem]
    scratch = [
        pltpu.VMEM((TABLE, C), F32),
        pltpu.VMEM((NODES, C), F32),
        pltpu.VMEM((E1, C), F32),
        pltpu.VMEM((1, E1), jnp.int32),
        pltpu.SMEM((1, E1), jnp.int32),
        pltpu.VMEM((2, 2, NHID, 512, 128), F32),
        pltpu.VMEM((2, NHID, 128, 512), F32),
        pltpu.VMEM((2, 3, 1536, 512), BF16),
        pltpu.VMEM((1024, 512), BF16),
        pltpu.VMEM((E1, NODES), BF16),
        pltpu.VMEM((NODES, E1), BF16),
        pltpu.VMEM((2 * E1, C), BF16),
        pltpu.VMEM((NHID, 2, 4, 128), F32),
        pltpu.VMEM((NHID, 2, 128), F32),
        pltpu.VMEM((16, C), F32),
        pltpu.VMEM((16, C), F32),
        pltpu.VMEM((3, 3, 1, 128), jnp.int32),
        pltpu.VMEM((3, 3, 128, C), F32),
        pltpu.VMEM((2, 3, 128, C), F32),
        pltpu.VMEM((2, 128, C), F32),
        pltpu.VMEM((2, 64, C), F32),
        pltpu.VMEM((NHID, 128, 128), F32),
        pltpu.VMEM((NHID, 128, 128), F32),
        pltpu.VMEM((NHID, NODES, 128), F32),
        dma((9,)),
        dma((2, 3, 3)), dma((2, 3, 3)),
        dma((2, 3, 3, 2)), dma((2, 3, 3, 2)),
        dma((2, 3, 3, 2)), dma((2, 3, 3, 2)),
        dma((14,)), dma((14,)),
        dma((3, 3)), dma((3, 3)),
        dma((2, 3, 2)), dma((2, 3, 2)),
        dma((3, 2)), dma((2, 2)),
        dma((3,)), dma((2,)),
        dma((3,)), dma((3,)),
    ]
    return pl.pallas_call(
        kernel,
        out_shape=jax.ShapeDtypeStruct((1, 1, NODES, 128), F32),
        in_specs=specs,
        out_specs=vmem,
        scratch_shapes=scratch,
        compiler_params=pltpu.CompilerParams(
            collective_id=0, has_side_effects=True, vmem_limit_bytes=56 * 2**20
        ),
        cost_estimate=pl.CostEstimate(flops=10**10, bytes_accessed=10**7, transcendentals=10**6),
    )(gl.reshape(GROWS * GCOLS, C), *rest)


def solution(mesh):
    return jax.shard_map(
        per_device,
        mesh=mesh,
        in_specs=(
            P("lat", "lon", None),
            P("lat", "lon", None, None),
            P("lat", "lon", None, None),
            P("lat", "lon", None),
            P("lat", "lon", None),
            P("lat", "lon", None, None),
            P("lat", "lon", None),
            P("lat", "lon", None),
            P(None, None, "hid"),
            P(None, None, "hid"),
            P(None, None, "hid"),
            P(None, "hid"),
            P(None, "hid", None),
            P(),
            P(),
            P(),
        ),
        out_specs=P("lat", "lon", None, "hid"),
        check_vma=False,
    )
```

```python
import jax
import jax.numpy as jnp
from jax import lax
from jax.experimental import pallas as pl
from jax.experimental.pallas import tpu as pltpu
from jax.sharding import PartitionSpec as P

MESH = pl.DeviceIdType.MESH
F32 = jnp.float32
BF16 = jnp.bfloat16
EPS = 1e-05
NLAT, NLON, NHID = 16, 8, 4
C = 512
NODES = 512
GROWS, GCOLS = 8, 128
E1, E2 = 1024, 512
Q2 = E2 // NHID
TABLE = 12 * GCOLS + 96
LEFT = 12 * GCOLS
RIGHT = LEFT + 48
RW, SW, OW = 0, 1, 2


def split(x):
    hi = x.astype(BF16)
    return hi, (x - hi.astype(F32)).astype(BF16)


def dot(a, b):
    return jnp.dot(a, b, preferred_element_type=F32)


def thrice(x):
    hi, lo = split(x)
    return jnp.concatenate([hi, hi, lo], axis=1)


def silu(t):
    return t / (1.0 + jnp.exp(-t))


def layer_norm(m, gain, shift):
    center = jnp.mean(m, axis=1, keepdims=True)
    d = m - center
    spread = jnp.mean(d * d, axis=1, keepdims=True)
    return d * lax.rsqrt(spread + EPS) * gain + shift


def kernel(
    gl, ml, gef, gs, gr, mef, ms, mr, ew, sw, rw, fb, ow, ob, ng, ns,
    out,
    table, mid, xs, idx_v, idx_s, wcol, wout, w3, r2, sel, agg, hidden, nrm, ewb, fbb, epack, wpack,
    req, gbuf, rlat, ry, rdiag, n1, rm, midb,
    load_sem, wx_s, wx_r, wy_s, wy_r, wc_s, wc_r, hx_s, hx_r, q_s, q_r, gl_s, gl_r, gy_s, gy_r,
    gd_s, gd_r, a_s, a_r,
):
    a = lax.axis_index("lat")
    b = lax.axis_index("lon")
    h = lax.axis_index("hid")
    core = lax.rem(a, 2)
    ypar = lax.rem(b, 2)
    sib = a + 1 - 2 * core
    zlat = lax.rem(a + NLAT - 1 + 2 * core, NLAT)
    lats = (zlat, sib, a)
    lons = (lax.rem(b + NLON - 1, NLON), b, lax.rem(b + 1, NLON))
    peers = [lax.rem(h + d, NHID) for d in (1, 2, 3)]
    patch = a * NLON + b

    def dev(group, q):
        return (lats[group], lons[q + 1], h)

    around = [(g, q) for g in range(3) for q in (-1, 0, 1) if not (g == 2 and q == 0)]

    barrier = pltpu.get_barrier_semaphore()
    for p in peers:
        pl.semaphore_signal(barrier, inc=1, device_id=(a, b, p), device_id_type=MESH)
    for g, q in around:
        pl.semaphore_signal(barrier, inc=1, device_id=dev(g, q), device_id_type=MESH)

    sent = []

    def send(src, dst, ssem, rsem, device):
        copy = pltpu.make_async_remote_copy(
            src_ref=src, dst_ref=dst, send_sem=ssem, recv_sem=rsem,
            device_id=device, device_id_type=MESH,
        )
        copy.start()
        sent.append(copy)

    def arrived(dst, rsem, device):
        pltpu.make_async_remote_copy(
            src_ref=dst, dst_ref=dst, send_sem=rsem, recv_sem=rsem,
            device_id=device, device_id_type=MESH,
        ).wait_recv()

    own_rows = table.at[pl.ds(2 * GCOLS, GROWS * GCOLS)]
    load_grid = pltpu.make_async_copy(gl, own_rows, load_sem.at[0])
    load_mesh = pltpu.make_async_copy(ml.at[0, 0], mid, load_sem.at[1])
    load_grid.start()
    load_mesh.start()
    own_loads = []
    for s in range(2):
        for i, (src, dst) in enumerate(
            ((rw.at[s], wcol.at[s, RW, h]), (sw.at[s], wcol.at[s, SW, h]), (ow.at[s], wout.at[s, h]))
        ):
            copy = pltpu.make_async_copy(src, dst, load_sem.at[2 + s * 3 + i])
            copy.start()
            own_loads.append(copy)

    ids = gs[0]
    lrow = lax.shift_right_logical(ids, 10) - a * GROWS + 2
    lcol = (lax.bitwise_and(ids, 1023) - b * GCOLS + 2 + 1024) & 1023
    side = (lrow + 6) * 2
    where = jnp.where(
        lcol < 2,
        LEFT + side + lcol,
        jnp.where(lcol >= GCOLS + 2, RIGHT + side + lcol - (GCOLS + 2), lrow * GCOLS + lcol - 2),
    )
    idx_v[...] = jnp.clip(where, 0, TABLE - 1)
    to_smem = pltpu.make_async_copy(idx_v, idx_s, load_sem.at[8])
    to_smem.start()

    pl.semaphore_wait(barrier, 11)

    low = table.at[pl.ds(0, 2 * GCOLS)]
    high = table.at[pl.ds(10 * GCOLS, 2 * GCOLS)]
    top = gl.at[pl.ds(6 * GCOLS, 2 * GCOLS)]
    bottom = gl.at[pl.ds(0, 2 * GCOLS)]
    up = lax.rem(a + 1, NLAT)
    down = lax.rem(a + NLAT - 1, NLAT)
    send(top, low, hx_s.at[0], hx_r.at[0], (up, b, h))
    send(bottom, high, hx_s.at[1], hx_r.at[1], (down, b, h))

    def src_of(s, m):
        return (rw, sw, ow)[m].at[s]

    def dst_of(s, m, who):
        return wout.at[s, who] if m == OW else wcol.at[s, m, who]

    def size_of(m):
        return 32 if m == OW else 128

    def piece(ref, m, which):
        n = size_of(m)
        return ref.at[pl.ds(pl.multiple_of(which * n, n), n)]

    def half(ref, m, which, part):
        n = size_of(m) // 2
        return ref.at[pl.ds(pl.multiple_of(which * 2 * n + part * n, n), n)]

    mine = 2 * core + ypar
    other = 2 * core + 1 - ypar
    sib_mine = 2 * (1 - core) + ypar
    sib_other = 2 * (1 - core) + 1 - ypar

    def x_send(s, m):
        for i, p in enumerate(peers):
            send(
                piece(src_of(s, m), m, mine), piece(dst_of(s, m, h), m, mine),
                wx_s.at[s, m, i], wx_r.at[s, m, i], (a, b, p),
            )

    def x_forward(s, m):
        for i in range(3):
            owner = peers[2 - i]
            arrived(piece(dst_of(s, m, owner), m, mine), wx_r.at[s, m, i], (a, b, owner))
            for part, q in ((0, 1), (1, -1)):
                view = half(dst_of(s, m, owner), m, mine, part)
                send(view, view, wy_s.at[s, m, i, part], wy_r.at[s, m, i, part], dev(2, q))
            view = piece(dst_of(s, m, owner), m, mine)
            send(view, view, wc_s.at[s, m, i, 0], wc_r.at[s, m, i, 0], dev(1, 0))

    def y_forward(s, m):
        for i in range(3):
            owner = peers[2 - i]
            for part, q in ((0, -1), (1, 1)):
                arrived(half(dst_of(s, m, owner), m, other, part), wy_r.at[s, m, i, part], dev(2, q))
            view = piece(dst_of(s, m, owner), m, other)
            send(view, view, wc_s.at[s, m, i, 1], wc_r.at[s, m, i, 1], dev(1, 0))

    def c_wait(s, m):
        for i in range(3):
            owner = peers[2 - i]
            arrived(piece(dst_of(s, m, owner), m, sib_mine), wc_r.at[s, m, i, 0], dev(1, 0))
            arrived(piece(dst_of(s, m, owner), m, sib_other), wc_r.at[s, m, i, 1], dev(1, 0))

    def build(s, m):
        own_loads[s * 3 + m].wait()
        for k in range(NHID):
            block = wout[s, k] if m == OW else wcol[s, m, k]
            hi, lo = split(block)
            if m == OW:
                for t, v in enumerate((hi, lo, hi)):
                    w3[s, m, pl.ds(t * 512 + k * 128, 128), :] = v
            else:
                for t, v in enumerate((hi, lo, hi)):
                    w3[s, m, pl.ds(t * 512, 512), pl.ds(k * 128, 128)] = v

    x_send(0, RW)
    for i, p in enumerate(peers):
        send(ew, ewb.at[h], hx_s.at[2 + i], hx_r.at[2 + i], (a, b, p))
        send(fb, fbb.at[h], hx_s.at[5 + i], hx_r.at[5 + i], (a, b, p))
    x_send(0, SW)
    x_send(0, OW)
    lanes = pl.ds(pl.multiple_of(h * Q2, Q2), Q2)
    for i, (g, q) in enumerate(around):
        send(ms.at[0, :, lanes], req.at[g, 1 - q], q_s.at[g, q + 1], q_r.at[g, 1 - q], dev(g, q))
    req[2, 1] = ms[0, :, lanes]
    ewb[h] = ew[...]
    fbb[h] = fb[...]

    load_grid.wait()
    for r in range(GROWS):
        base = (2 + r) * GCOLS
        wpack[pl.ds(2 * r, 2), :] = table[pl.ds(base, 2), :]
        epack[pl.ds(2 * r, 2), :] = table[pl.ds(base + GCOLS - 2, 2), :]
    for j, g in enumerate((0, 1, 2)):
        if g == 0:
            seg_at_target = 32 * (1 - core)
        elif g == 1:
            seg_at_target = 32 * core
        else:
            seg_at_target = 16
        for side_i, (pack, base, q) in enumerate(((epack, LEFT, 1), (wpack, RIGHT, -1))):
            send(
                pack, table.at[pl.ds(pl.multiple_of(base + seg_at_target, 16), 16)],
                hx_s.at[8 + 2 * j + side_i], hx_r.at[8 + 2 * j + side_i], dev(g, q),
            )

    x_forward(0, RW)
    x_send(1, SW)

    local = (gr[0] - patch * NODES).astype(F32)
    node_rows = lax.broadcasted_iota(jnp.int32, (NODES, 128), 0).astype(F32)
    node_lanes = lax.broadcasted_iota(jnp.int32, (128, NODES), 1).astype(F32)

    def agg_block(row):
        return jnp.where(node_rows == row, 1.0, 0.0).astype(BF16)

    def sel_block(row):
        col = jnp.transpose(jnp.broadcast_to(row, (128, 128)))
        return jnp.where(node_lanes == jnp.concatenate([col] * 4, axis=1), 1.0, 0.0).astype(BF16)

    for j in range(E1 // 128):
        row = local[:, j * 128 : (j + 1) * 128]
        agg[:, pl.ds(j * 128, 128)] = agg_block(row)
        sel[pl.ds(j * 128, 128), :] = sel_block(row)

    x_forward(0, SW)
    y_forward(0, RW)
    x_forward(0, OW)
    y_forward(0, SW)
    to_smem.wait()
    arrived(low, hx_r.at[0], (down, b, h))
    arrived(high, hx_r.at[1], (up, b, h))
    for j, g in enumerate((0, 1, 2)):
        if g == 0:
            seg = 32 * core
        elif g == 1:
            seg = 32 * (1 - core)
        else:
            seg = 16
        for side_i, (base, q) in enumerate(((LEFT, -1), (RIGHT, 1))):
            arrived(
                table.at[pl.ds(pl.multiple_of(base + seg, 16), 16)],
                hx_r.at[8 + 2 * j + side_i], dev(g, q),
            )

    def take_rows(i, carry):
        for k in range(8):
            e = i * 8 + k
            xs[pl.ds(e, 1), :] = table[pl.ds(idx_s[0, e], 1), :]
        return carry

    lax.fori_loop(0, E1 // 8, take_rows, 0)

    for i in range(3):
        arrived(ewb.at[peers[2 - i]], hx_r.at[2 + i], (a, b, peers[2 - i]))
        arrived(fbb.at[peers[2 - i]], hx_r.at[5 + i], (a, b, peers[2 - i]))

    def edge_weights(s):
        w = jnp.concatenate([ewb[k, s] for k in range(NHID)], axis=1)
        bias = jnp.concatenate([fbb[k, pl.ds(s, 1)] for k in range(NHID)], axis=1)
        wh = w.astype(BF16).astype(F32)
        bh = bias.astype(BF16).astype(F32)
        bl = (bias - bh).astype(BF16).astype(F32)
        bll = bias - bh - bl
        rows = [wh, w - wh, wh, bh, bl, bll, jnp.zeros_like(bll)]
        return jnp.concatenate(rows, axis=0).astype(BF16)

    def edge_feats(f):
        fh = f.astype(BF16).astype(F32)
        rows = [fh, fh, f - fh, jnp.ones_like(f)]
        return jnp.transpose(jnp.concatenate(rows, axis=0)).astype(BF16)

    ew0 = edge_weights(0)

    load_mesh.wait()
    c_wait(0, RW)
    build(0, RW)
    y_forward(0, OW)
    terms = dot(thrice(mid[...]), w3[0, RW])
    hi, lo = split(terms)
    r2[pl.ds(0, 512), :] = hi
    r2[pl.ds(512, 512), :] = lo

    c_wait(0, SW)
    build(0, SW)
    x_forward(1, SW)
    x_send(1, RW)
    x_send(1, OW)

    STEP = 256
    for j in range(E1 // STEP):
        rows = pl.ds(j * STEP, STEP)
        one = sel[rows, :]
        pre = dot(thrice(xs[rows, :]), w3[0, SW])
        pre += dot(jnp.concatenate([one, one], axis=1), r2[...])
        pre += dot(edge_feats(gef[0, 0, :, j * STEP : (j + 1) * STEP]), ew0)
        hidden[0, rows, :], hidden[1, rows, :] = split(silu(pre))
        if j == 1:
            y_forward(1, SW)
    c_wait(0, OW)
    build(0, OW)
    for j in range(E1 // STEP):
        rows = pl.ds(j * STEP, STEP)
        hi, lo = hidden[0, rows, :], hidden[1, rows, :]
        message = dot(jnp.concatenate([hi, hi, lo], axis=1), w3[0, OW]) + ob[pl.ds(0, 1), :]
        hi, lo = split(layer_norm(message, ng[pl.ds(0, 1), :], ns[pl.ds(0, 1), :]))
        nrm[rows, :] = hi
        nrm[pl.ds(E1 + j * STEP, STEP), :] = lo
        if j == 1:
            x_forward(1, RW)
        if j == 3:
            x_forward(1, OW)

    both = agg[...]
    mid[...] += dot(jnp.concatenate([both, both], axis=1), nrm[...])
    c_wait(1, SW)
    build(1, SW)
    mid3 = thrice(mid[...])
    hi, lo = split(dot(mid3, w3[1, SW]))
    r2[pl.ds(0, 512), :] = hi
    r2[pl.ds(512, 512), :] = lo

    for i, (g, q) in enumerate(around):
        arrived(req.at[g, q + 1], q_r.at[g, q + 1], dev(g, q))

    def contributions(g):
        picks = [sel_block((req[g, t] - patch * NODES).astype(F32)) for t in range(3)]
        picks = jnp.concatenate(picks, axis=0)
        found = dot(jnp.concatenate([picks, picks], axis=1), r2[...])
        for t in range(3):
            gbuf[g, t] = found[t * 128 : (t + 1) * 128]

    first, second = pl.ds(0, 64), pl.ds(64, 64)
    contributions(0)
    for t, q in ((0, -1), (2, 1)):
        send(gbuf.at[0, t, first], rlat.at[0, t, first], gl_s.at[0, t, 0], gl_r.at[0, t, 0], dev(0, 0))
        side_i = 1 if q < 0 else 0
        send(gbuf.at[0, t, second], rdiag.at[side_i], gd_s.at[t], gd_r.at[side_i], dev(2, q))
    send(gbuf.at[0, 1, first], rlat.at[0, 1, first], gl_s.at[0, 1, 0], gl_r.at[0, 1, 0], dev(0, 0))
    contributions(1)
    for t in (0, 2, 1):
        send(gbuf.at[1, t], rlat.at[1, t], gl_s.at[1, t, 0], gl_r.at[1, t, 0], dev(1, 0))
    contributions(2)
    for t, q in ((0, -1), (2, 1)):
        arrived(rlat.at[1, t], gl_r.at[1, t, 0], dev(1, 0))
        gbuf[2, t] = gbuf[2, t] + rlat[1, t]
        side_i = 1 if q < 0 else 0
        send(gbuf.at[2, t, second], ry.at[side_i, second], gy_s.at[t, 1], gy_r.at[side_i, 1], dev(2, q))
    arrived(rdiag.at[1], gd_r.at[1], dev(2, 1))
    arrived(rdiag.at[0], gd_r.at[0], dev(2, -1))
    gbuf[0, 1, second] = gbuf[0, 1, second] + rdiag[0] + rdiag[1]
    send(gbuf.at[0, 1, second], rlat.at[0, 1, second], gl_s.at[0, 1, 1], gl_r.at[0, 1, 1], dev(0, 0))
    for t, q in ((0, -1), (2, 1)):
        arrived(rlat.at[0, t, first], gl_r.at[0, t, 0], dev(0, 0))
        gbuf[2, t, first] = gbuf[2, t, first] + rlat[0, t, first]
        side_i = 1 if q < 0 else 0
        send(gbuf.at[2, t, first], ry.at[side_i, first], gy_s.at[t, 0], gy_r.at[side_i, 0], dev(2, q))
    y_forward(1, RW)
    y_forward(1, OW)
    for m in (RW, OW):
        c_wait(1, m)
        build(1, m)
    local2 = (mr[0] - patch * NODES).astype(F32)
    for j in range(E2 // 128):
        agg[:, pl.ds(j * 128, 128)] = agg_block(local2[:, j * 128 : (j + 1) * 128])
    for k in range(NHID):
        midb[k] = mid[:, k * 128 : (k + 1) * 128]
    mine_recv = (mr[0, :, lanes] - patch * NODES).astype(F32)
    one = sel_block(mine_recv)
    mh, mlo = split(mid[...])
    picked = dot(one, mh) + dot(one, mlo)
    pre = dot(thrice(picked), w3[1, RW]) + dot(edge_feats(mef[0, 0, :, lanes]), edge_weights(1))

    pre += gbuf[2, 1]
    arrived(rlat.at[1, 1], gl_r.at[1, 1, 0], dev(1, 0))
    for part, rows in ((1, second), (0, first)):
        arrived(rlat.at[0, 1, rows], gl_r.at[0, 1, part], dev(0, 0))
        arrived(ry.at[1, rows], gy_r.at[1, part], dev(2, 1))
        arrived(ry.at[0, rows], gy_r.at[0, part], dev(2, -1))
        t = pre[part * 64 : part * 64 + 64]
        t = t + rlat[1, 1, rows] + rlat[0, 1, rows] + ry[0, rows] + ry[1, rows]
        message = dot(thrice(silu(t)), w3[1, OW]) + ob[pl.ds(1, 1), :]
        normed = layer_norm(message, ng[pl.ds(1, 1), :], ns[pl.ds(1, 1), :])
        for k in range(NHID):
            n1[k, rows] = normed[:, k * 128 : (k + 1) * 128]
        for i, p in enumerate(peers):
            send(n1.at[p, rows], rm.at[h, rows], a_s.at[part, i], a_r.at[part, i], (a, b, p))
    rm[h] = n1[h]
    for part, rows in ((1, second), (0, first)):
        for i in range(3):
            owner = peers[2 - i]
            arrived(rm.at[owner, rows], a_r.at[part, i], (a, b, owner))
    hi, lo = split(rm[...].reshape(E2, 128))
    one = agg[:, pl.ds(0, E2)]
    out[0, 0] = midb[h] + dot(one, hi) + dot(one, lo)
    for copy in sent:
        copy.wait_send()


def per_device(gl, *rest):
    dma = pltpu.SemaphoreType.DMA
    vmem = pl.BlockSpec(memory_space=pltpu.VMEM)
    hbm = pl.BlockSpec(memory_space=pl.ANY)
    specs = [hbm, hbm, vmem, vmem, vmem, vmem, vmem, vmem, vmem, hbm, hbm, vmem, hbm, vmem, vmem, vmem]
    scratch = [
        pltpu.VMEM((TABLE, C), F32),
        pltpu.VMEM((NODES, C), F32),
        pltpu.VMEM((E1, C), F32),
        pltpu.VMEM((1, E1), jnp.int32),
        pltpu.SMEM((1, E1), jnp.int32),
        pltpu.VMEM((2, 2, NHID, 512, 128), F32),
        pltpu.VMEM((2, NHID, 128, 512), F32),
        pltpu.VMEM((2, 3, 1536, 512), BF16),
        pltpu.VMEM((1024, 512), BF16),
        pltpu.VMEM((E1, NODES), BF16),
        pltpu.VMEM((NODES, E1), BF16),
        pltpu.VMEM((2, E1, C), BF16),
        pltpu.VMEM((2 * E1, C), BF16),
        pltpu.VMEM((NHID, 2, 4, 128), F32),
        pltpu.VMEM((NHID, 2, 128), F32),
        pltpu.VMEM((16, C), F32),
        pltpu.VMEM((16, C), F32),
        pltpu.VMEM((3, 3, 1, 128), jnp.int32),
        pltpu.VMEM((3, 3, 128, C), F32),
        pltpu.VMEM((2, 3, 128, C), F32),
        pltpu.VMEM((2, 128, C), F32),
        pltpu.VMEM((2, 64, C), F32),
        pltpu.VMEM((NHID, 128, 128), F32),
        pltpu.VMEM((NHID, 128, 128), F32),
        pltpu.VMEM((NHID, NODES, 128), F32),
        dma((9,)),
        dma((2, 3, 3)), dma((2, 3, 3)),
        dma((2, 3, 3, 2)), dma((2, 3, 3, 2)),
        dma((2, 3, 3, 2)), dma((2, 3, 3, 2)),
        dma((14,)), dma((14,)),
        dma((3, 3)), dma((3, 3)),
        dma((2, 3, 2)), dma((2, 3, 2)),
        dma((3, 2)), dma((2, 2)),
        dma((3,)), dma((2,)),
        dma((2, 3)), dma((2, 3)),
    ]
    return pl.pallas_call(
        kernel,
        out_shape=jax.ShapeDtypeStruct((1, 1, NODES, 128), F32),
        in_specs=specs,
        out_specs=vmem,
        scratch_shapes=scratch,
        compiler_params=pltpu.CompilerParams(
            collective_id=0, has_side_effects=True, vmem_limit_bytes=56 * 2**20
        ),
        cost_estimate=pl.CostEstimate(flops=10**10, bytes_accessed=10**7, transcendentals=10**6),
    )(gl.reshape(GROWS * GCOLS, C), *rest)


def solution(mesh):
    return jax.shard_map(
        per_device,
        mesh=mesh,
        in_specs=(
            P("lat", "lon", None),
            P("lat", "lon", None, None),
            P("lat", "lon", None, None),
            P("lat", "lon", None),
            P("lat", "lon", None),
            P("lat", "lon", None, None),
            P("lat", "lon", None),
            P("lat", "lon", None),
            P(None, None, "hid"),
            P(None, None, "hid"),
            P(None, None, "hid"),
            P(None, "hid"),
            P(None, "hid", None),
            P(),
            P(),
            P(),
        ),
        out_specs=P("lat", "lon", None, "hid"),
        check_vma=False,
    )
```

```python
import jax
import jax.numpy as jnp
from jax import lax
from jax.experimental import pallas as pl
from jax.experimental.pallas import tpu as pltpu
from jax.sharding import PartitionSpec as P

MESH = pl.DeviceIdType.MESH
F32 = jnp.float32
BF16 = jnp.bfloat16
EPS = 1e-05
NLAT, NLON, NHID = 16, 8, 4
C = 512
NODES = 512
GROWS, GCOLS = 8, 128
E1, E2 = 1024, 512
Q2 = E2 // NHID
TABLE = 12 * GCOLS + 96
LEFT = 12 * GCOLS
RIGHT = LEFT + 48
RW, SW, OW = 0, 1, 2


def split(x):
    hi = x.astype(BF16)
    return hi, (x - hi.astype(F32)).astype(BF16)


def dot(a, b):
    return jnp.dot(a, b, preferred_element_type=F32)


def thrice(x):
    hi, lo = split(x)
    return jnp.concatenate([hi, hi, lo], axis=1)


def silu(t):
    return t / (1.0 + jnp.exp(-t))


def layer_norm(m, gain, shift):
    center = jnp.mean(m, axis=1, keepdims=True)
    d = m - center
    spread = jnp.mean(d * d, axis=1, keepdims=True)
    return d * lax.rsqrt(spread + EPS) * gain + shift


def kernel(
    gl, ml, gef, gs, gr, mef, ms, mr, ew, sw, rw, fb, ow, ob, ng, ns,
    out,
    table, mid, xs, idx_v, idx_s, wcol, wout, w3, r2, sel, agg, hidden, nrm, ewb, fbb, epack, wpack,
    req, gbuf, rlat, ry, rdiag, n1, rm, midb,
    load_sem, wx_s, wx_r, wy_s, wy_r, wc_s, wc_r, hx_s, hx_r, q_s, q_r, gl_s, gl_r, gy_s, gy_r,
    gd_s, gd_r, a_s, a_r,
):
    a = lax.axis_index("lat")
    b = lax.axis_index("lon")
    h = lax.axis_index("hid")
    core = lax.rem(a, 2)
    ypar = lax.rem(b, 2)
    sib = a + 1 - 2 * core
    zlat = lax.rem(a + NLAT - 1 + 2 * core, NLAT)
    lats = (zlat, sib, a)
    lons = (lax.rem(b + NLON - 1, NLON), b, lax.rem(b + 1, NLON))
    peers = [lax.rem(h + d, NHID) for d in (1, 2, 3)]
    patch = a * NLON + b

    def dev(group, q):
        return (lats[group], lons[q + 1], h)

    around = [(g, q) for g in range(3) for q in (-1, 0, 1) if not (g == 2 and q == 0)]

    barrier = pltpu.get_barrier_semaphore()
    for p in peers:
        pl.semaphore_signal(barrier, inc=1, device_id=(a, b, p), device_id_type=MESH)
    for g, q in around:
        pl.semaphore_signal(barrier, inc=1, device_id=dev(g, q), device_id_type=MESH)

    sent = []

    def send(src, dst, ssem, rsem, device):
        copy = pltpu.make_async_remote_copy(
            src_ref=src, dst_ref=dst, send_sem=ssem, recv_sem=rsem,
            device_id=device, device_id_type=MESH,
        )
        copy.start()
        sent.append(copy)

    def arrived(dst, rsem, device):
        pltpu.make_async_remote_copy(
            src_ref=dst, dst_ref=dst, send_sem=rsem, recv_sem=rsem,
            device_id=device, device_id_type=MESH,
        ).wait_recv()

    own_rows = table.at[pl.ds(2 * GCOLS, GROWS * GCOLS)]
    load_grid = pltpu.make_async_copy(gl, own_rows, load_sem.at[0])
    load_mesh = pltpu.make_async_copy(ml.at[0, 0], mid, load_sem.at[1])
    load_grid.start()
    load_mesh.start()
    own_loads = []
    for s in range(2):
        for i, (src, dst) in enumerate(
            ((rw.at[s], wcol.at[s, RW, h]), (sw.at[s], wcol.at[s, SW, h]), (ow.at[s], wout.at[s, h]))
        ):
            copy = pltpu.make_async_copy(src, dst, load_sem.at[2 + s * 3 + i])
            copy.start()
            own_loads.append(copy)

    ids = gs[0]
    lrow = lax.shift_right_logical(ids, 10) - a * GROWS + 2
    lcol = (lax.bitwise_and(ids, 1023) - b * GCOLS + 2 + 1024) & 1023
    side = (lrow + 6) * 2
    where = jnp.where(
        lcol < 2,
        LEFT + side + lcol,
        jnp.where(lcol >= GCOLS + 2, RIGHT + side + lcol - (GCOLS + 2), lrow * GCOLS + lcol - 2),
    )
    idx_v[...] = jnp.clip(where, 0, TABLE - 1)
    to_smem = pltpu.make_async_copy(idx_v, idx_s, load_sem.at[8])
    to_smem.start()

    pl.semaphore_wait(barrier, 11)

    low = table.at[pl.ds(0, 2 * GCOLS)]
    high = table.at[pl.ds(10 * GCOLS, 2 * GCOLS)]
    top = gl.at[pl.ds(6 * GCOLS, 2 * GCOLS)]
    bottom = gl.at[pl.ds(0, 2 * GCOLS)]
    up = lax.rem(a + 1, NLAT)
    down = lax.rem(a + NLAT - 1, NLAT)
    send(top, low, hx_s.at[0], hx_r.at[0], (up, b, h))
    send(bottom, high, hx_s.at[1], hx_r.at[1], (down, b, h))

    def src_of(s, m):
        return (rw, sw, ow)[m].at[s]

    def dst_of(s, m, who):
        return wout.at[s, who] if m == OW else wcol.at[s, m, who]

    def size_of(m):
        return 32 if m == OW else 128

    def piece(ref, m, which):
        n = size_of(m)
        return ref.at[pl.ds(pl.multiple_of(which * n, n), n)]

    def half(ref, m, which, part):
        n = size_of(m) // 2
        return ref.at[pl.ds(pl.multiple_of(which * 2 * n + part * n, n), n)]

    mine = 2 * core + ypar
    other = 2 * core + 1 - ypar
    sib_mine = 2 * (1 - core) + ypar
    sib_other = 2 * (1 - core) + 1 - ypar

    def x_send(s, m):
        for i, p in enumerate(peers):
            send(
                piece(src_of(s, m), m, mine), piece(dst_of(s, m, h), m, mine),
                wx_s.at[s, m, i], wx_r.at[s, m, i], (a, b, p),
            )

    def x_forward(s, m):
        for i in range(3):
            owner = peers[2 - i]
            arrived(piece(dst_of(s, m, owner), m, mine), wx_r.at[s, m, i], (a, b, owner))
            for part, q in ((0, 1), (1, -1)):
                view = half(dst_of(s, m, owner), m, mine, part)
                send(view, view, wy_s.at[s, m, i, part], wy_r.at[s, m, i, part], dev(2, q))
            view = piece(dst_of(s, m, owner), m, mine)
            send(view, view, wc_s.at[s, m, i, 0], wc_r.at[s, m, i, 0], dev(1, 0))

    def y_forward(s, m):
        for i in range(3):
            owner = peers[2 - i]
            for part, q in ((0, -1), (1, 1)):
                arrived(half(dst_of(s, m, owner), m, other, part), wy_r.at[s, m, i, part], dev(2, q))
            view = piece(dst_of(s, m, owner), m, other)
            send(view, view, wc_s.at[s, m, i, 1], wc_r.at[s, m, i, 1], dev(1, 0))

    def c_wait(s, m):
        for i in range(3):
            owner = peers[2 - i]
            arrived(piece(dst_of(s, m, owner), m, sib_mine), wc_r.at[s, m, i, 0], dev(1, 0))
            arrived(piece(dst_of(s, m, owner), m, sib_other), wc_r.at[s, m, i, 1], dev(1, 0))

    def build(s, m):
        own_loads[s * 3 + m].wait()
        for k in range(NHID):
            block = wout[s, k] if m == OW else wcol[s, m, k]
            hi, lo = split(block)
            if m == OW:
                for t, v in enumerate((hi, lo, hi)):
                    w3[s, m, pl.ds(t * 512 + k * 128, 128), :] = v
            else:
                for t, v in enumerate((hi, lo, hi)):
                    w3[s, m, pl.ds(t * 512, 512), pl.ds(k * 128, 128)] = v

    x_send(0, RW)
    for i, p in enumerate(peers):
        send(ew, ewb.at[h], hx_s.at[2 + i], hx_r.at[2 + i], (a, b, p))
        send(fb, fbb.at[h], hx_s.at[5 + i], hx_r.at[5 + i], (a, b, p))
    x_send(0, SW)
    x_send(0, OW)
    lanes = pl.ds(pl.multiple_of(h * Q2, Q2), Q2)
    for i, (g, q) in enumerate(around):
        send(ms.at[0, :, lanes], req.at[g, 1 - q], q_s.at[g, q + 1], q_r.at[g, 1 - q], dev(g, q))
    req[2, 1] = ms[0, :, lanes]
    ewb[h] = ew[...]
    fbb[h] = fb[...]

    load_grid.wait()
    for r in range(GROWS):
        base = (2 + r) * GCOLS
        wpack[pl.ds(2 * r, 2), :] = table[pl.ds(base, 2), :]
        epack[pl.ds(2 * r, 2), :] = table[pl.ds(base + GCOLS - 2, 2), :]
    for j, g in enumerate((0, 1, 2)):
        if g == 0:
            seg_at_target = 32 * (1 - core)
        elif g == 1:
            seg_at_target = 32 * core
        else:
            seg_at_target = 16
        for side_i, (pack, base, q) in enumerate(((epack, LEFT, 1), (wpack, RIGHT, -1))):
            send(
                pack, table.at[pl.ds(pl.multiple_of(base + seg_at_target, 16), 16)],
                hx_s.at[8 + 2 * j + side_i], hx_r.at[8 + 2 * j + side_i], dev(g, q),
            )

    x_forward(0, RW)
    x_send(1, SW)

    local = (gr[0] - patch * NODES).astype(F32)
    node_rows = lax.broadcasted_iota(jnp.int32, (NODES, 128), 0).astype(F32)
    node_lanes = lax.broadcasted_iota(jnp.int32, (128, NODES), 1).astype(F32)

    def agg_block(row):
        return jnp.where(node_rows == row, 1.0, 0.0).astype(BF16)

    def sel_block(row):
        col = jnp.transpose(jnp.broadcast_to(row, (128, 128)))
        return jnp.where(node_lanes == jnp.concatenate([col] * 4, axis=1), 1.0, 0.0).astype(BF16)

    for j in range(E1 // 128):
        row = local[:, j * 128 : (j + 1) * 128]
        agg[:, pl.ds(j * 128, 128)] = agg_block(row)
        sel[pl.ds(j * 128, 128), :] = sel_block(row)

    x_forward(0, SW)
    y_forward(0, RW)
    x_forward(0, OW)
    y_forward(0, SW)
    to_smem.wait()
    arrived(low, hx_r.at[0], (down, b, h))
    arrived(high, hx_r.at[1], (up, b, h))
    for j, g in enumerate((0, 1, 2)):
        if g == 0:
            seg = 32 * core
        elif g == 1:
            seg = 32 * (1 - core)
        else:
            seg = 16
        for side_i, (base, q) in enumerate(((LEFT, -1), (RIGHT, 1))):
            arrived(
                table.at[pl.ds(pl.multiple_of(base + seg, 16), 16)],
                hx_r.at[8 + 2 * j + side_i], dev(g, q),
            )

    def take_rows(i, carry):
        for k in range(8):
            e = i * 8 + k
            xs[pl.ds(e, 1), :] = table[pl.ds(idx_s[0, e], 1), :]
        return carry

    lax.fori_loop(0, E1 // 8, take_rows, 0)

    for i in range(3):
        arrived(ewb.at[peers[2 - i]], hx_r.at[2 + i], (a, b, peers[2 - i]))
        arrived(fbb.at[peers[2 - i]], hx_r.at[5 + i], (a, b, peers[2 - i]))

    def edge_weights(s):
        w = jnp.concatenate([ewb[k, s] for k in range(NHID)], axis=1)
        bias = jnp.concatenate([fbb[k, pl.ds(s, 1)] for k in range(NHID)], axis=1)
        wh = w.astype(BF16).astype(F32)
        bh = bias.astype(BF16).astype(F32)
        bl = (bias - bh).astype(BF16).astype(F32)
        bll = bias - bh - bl
        rows = [wh, w - wh, wh, bh, bl, bll, jnp.zeros_like(bll)]
        return jnp.concatenate(rows, axis=0).astype(BF16)

    def edge_feats(f):
        fh = f.astype(BF16).astype(F32)
        rows = [fh, fh, f - fh, jnp.ones_like(f)]
        return jnp.transpose(jnp.concatenate(rows, axis=0)).astype(BF16)

    ew0 = edge_weights(0)

    load_mesh.wait()
    c_wait(0, RW)
    build(0, RW)
    terms = dot(thrice(mid[...]), w3[0, RW])
    hi, lo = split(terms)
    r2[pl.ds(0, 512), :] = hi
    r2[pl.ds(512, 512), :] = lo

    c_wait(0, SW)
    build(0, SW)
    y_forward(0, OW)

    STEP = 256
    for j in range(E1 // STEP):
        rows = pl.ds(j * STEP, STEP)
        one = sel[rows, :]
        pre = dot(thrice(xs[rows, :]), w3[0, SW])
        pre += dot(jnp.concatenate([one, one], axis=1), r2[...])
        pre += dot(edge_feats(gef[0, 0, :, j * STEP : (j + 1) * STEP]), ew0)
        hidden[0, rows, :], hidden[1, rows, :] = split(silu(pre))
        if j == 0:
            x_forward(1, SW)
            x_send(1, RW)
            x_send(1, OW)
        if j == 3:
            y_forward(1, SW)
    c_wait(0, OW)
    build(0, OW)
    for j in range(E1 // STEP):
        rows = pl.ds(j * STEP, STEP)
        hi, lo = hidden[0, rows, :], hidden[1, rows, :]
        message = dot(jnp.concatenate([hi, hi, lo], axis=1), w3[0, OW]) + ob[pl.ds(0, 1), :]
        hi, lo = split(layer_norm(message, ng[pl.ds(0, 1), :], ns[pl.ds(0, 1), :]))
        nrm[rows, :] = hi
        nrm[pl.ds(E1 + j * STEP, STEP), :] = lo
        if j == 1:
            x_forward(1, RW)
        if j == 3:
            x_forward(1, OW)

    both = agg[...]
    mid[...] += dot(jnp.concatenate([both, both], axis=1), nrm[...])
    c_wait(1, SW)
    build(1, SW)
    mid3 = thrice(mid[...])
    hi, lo = split(dot(mid3, w3[1, SW]))
    r2[pl.ds(0, 512), :] = hi
    r2[pl.ds(512, 512), :] = lo

    for i, (g, q) in enumerate(around):
        arrived(req.at[g, q + 1], q_r.at[g, q + 1], dev(g, q))

    def contributions(g):
        picks = [sel_block((req[g, t] - patch * NODES).astype(F32)) for t in range(3)]
        picks = jnp.concatenate(picks, axis=0)
        found = dot(jnp.concatenate([picks, picks], axis=1), r2[...])
        for t in range(3):
            gbuf[g, t] = found[t * 128 : (t + 1) * 128]

    first, second = pl.ds(0, 64), pl.ds(64, 64)
    contributions(0)
    for t, q in ((0, -1), (2, 1)):
        send(gbuf.at[0, t, first], rlat.at[0, t, first], gl_s.at[0, t, 0], gl_r.at[0, t, 0], dev(0, 0))
        side_i = 1 if q < 0 else 0
        send(gbuf.at[0, t, second], rdiag.at[side_i], gd_s.at[t], gd_r.at[side_i], dev(2, q))
    send(gbuf.at[0, 1, first], rlat.at[0, 1, first], gl_s.at[0, 1, 0], gl_r.at[0, 1, 0], dev(0, 0))
    contributions(1)
    for t in (0, 2, 1):
        send(gbuf.at[1, t], rlat.at[1, t], gl_s.at[1, t, 0], gl_r.at[1, t, 0], dev(1, 0))
    contributions(2)
    for t, q in ((0, -1), (2, 1)):
        arrived(rlat.at[1, t], gl_r.at[1, t, 0], dev(1, 0))
        gbuf[2, t] = gbuf[2, t] + rlat[1, t]
        side_i = 1 if q < 0 else 0
        send(gbuf.at[2, t, second], ry.at[side_i, second], gy_s.at[t, 1], gy_r.at[side_i, 1], dev(2, q))
    arrived(rdiag.at[1], gd_r.at[1], dev(2, 1))
    arrived(rdiag.at[0], gd_r.at[0], dev(2, -1))
    gbuf[0, 1, second] = gbuf[0, 1, second] + rdiag[0] + rdiag[1]
    send(gbuf.at[0, 1, second], rlat.at[0, 1, second], gl_s.at[0, 1, 1], gl_r.at[0, 1, 1], dev(0, 0))
    for t, q in ((0, -1), (2, 1)):
        arrived(rlat.at[0, t, first], gl_r.at[0, t, 0], dev(0, 0))
        gbuf[2, t, first] = gbuf[2, t, first] + rlat[0, t, first]
        side_i = 1 if q < 0 else 0
        send(gbuf.at[2, t, first], ry.at[side_i, first], gy_s.at[t, 0], gy_r.at[side_i, 0], dev(2, q))
    y_forward(1, RW)
    y_forward(1, OW)
    for m in (RW, OW):
        c_wait(1, m)
        build(1, m)
    local2 = (mr[0] - patch * NODES).astype(F32)
    for j in range(E2 // 128):
        agg[:, pl.ds(j * 128, 128)] = agg_block(local2[:, j * 128 : (j + 1) * 128])
    for k in range(NHID):
        midb[k] = mid[:, k * 128 : (k + 1) * 128]
    mine_recv = (mr[0, :, lanes] - patch * NODES).astype(F32)
    one = sel_block(mine_recv)
    mh, mlo = split(mid[...])
    picked = dot(one, mh) + dot(one, mlo)
    pre = dot(thrice(picked), w3[1, RW]) + dot(edge_feats(mef[0, 0, :, lanes]), edge_weights(1))

    pre += gbuf[2, 1]
    arrived(rlat.at[1, 1], gl_r.at[1, 1, 0], dev(1, 0))
    for part, rows in ((1, second), (0, first)):
        arrived(rlat.at[0, 1, rows], gl_r.at[0, 1, part], dev(0, 0))
        arrived(ry.at[1, rows], gy_r.at[1, part], dev(2, 1))
        arrived(ry.at[0, rows], gy_r.at[0, part], dev(2, -1))
        t = pre[part * 64 : part * 64 + 64]
        t = t + rlat[1, 1, rows] + rlat[0, 1, rows] + ry[0, rows] + ry[1, rows]
        message = dot(thrice(silu(t)), w3[1, OW]) + ob[pl.ds(1, 1), :]
        normed = layer_norm(message, ng[pl.ds(1, 1), :], ns[pl.ds(1, 1), :])
        for k in range(NHID):
            n1[k, rows] = normed[:, k * 128 : (k + 1) * 128]
        for i, p in enumerate(peers):
            send(n1.at[p, rows], rm.at[h, rows], a_s.at[part, i], a_r.at[part, i], (a, b, p))
    rm[h] = n1[h]
    for part, rows in ((1, second), (0, first)):
        for i in range(3):
            owner = peers[2 - i]
            arrived(rm.at[owner, rows], a_r.at[part, i], (a, b, owner))
    hi, lo = split(rm[...].reshape(E2, 128))
    one = agg[:, pl.ds(0, E2)]
    out[0, 0] = midb[h] + dot(one, hi) + dot(one, lo)
    for copy in sent:
        copy.wait_send()


def per_device(gl, *rest):
    dma = pltpu.SemaphoreType.DMA
    vmem = pl.BlockSpec(memory_space=pltpu.VMEM)
    hbm = pl.BlockSpec(memory_space=pl.ANY)
    specs = [hbm, hbm, vmem, vmem, vmem, vmem, vmem, vmem, vmem, hbm, hbm, vmem, hbm, vmem, vmem, vmem]
    scratch = [
        pltpu.VMEM((TABLE, C), F32),
        pltpu.VMEM((NODES, C), F32),
        pltpu.VMEM((E1, C), F32),
        pltpu.VMEM((1, E1), jnp.int32),
        pltpu.SMEM((1, E1), jnp.int32),
        pltpu.VMEM((2, 2, NHID, 512, 128), F32),
        pltpu.VMEM((2, NHID, 128, 512), F32),
        pltpu.VMEM((2, 3, 1536, 512), BF16),
        pltpu.VMEM((1024, 512), BF16),
        pltpu.VMEM((E1, NODES), BF16),
        pltpu.VMEM((NODES, E1), BF16),
        pltpu.VMEM((2, E1, C), BF16),
        pltpu.VMEM((2 * E1, C), BF16),
        pltpu.VMEM((NHID, 2, 4, 128), F32),
        pltpu.VMEM((NHID, 2, 128), F32),
        pltpu.VMEM((16, C), F32),
        pltpu.VMEM((16, C), F32),
        pltpu.VMEM((3, 3, 1, 128), jnp.int32),
        pltpu.VMEM((3, 3, 128, C), F32),
        pltpu.VMEM((2, 3, 128, C), F32),
        pltpu.VMEM((2, 128, C), F32),
        pltpu.VMEM((2, 64, C), F32),
        pltpu.VMEM((NHID, 128, 128), F32),
        pltpu.VMEM((NHID, 128, 128), F32),
        pltpu.VMEM((NHID, NODES, 128), F32),
        dma((9,)),
        dma((2, 3, 3)), dma((2, 3, 3)),
        dma((2, 3, 3, 2)), dma((2, 3, 3, 2)),
        dma((2, 3, 3, 2)), dma((2, 3, 3, 2)),
        dma((14,)), dma((14,)),
        dma((3, 3)), dma((3, 3)),
        dma((2, 3, 2)), dma((2, 3, 2)),
        dma((3, 2)), dma((2, 2)),
        dma((3,)), dma((2,)),
        dma((2, 3)), dma((2, 3)),
    ]
    return pl.pallas_call(
        kernel,
        out_shape=jax.ShapeDtypeStruct((1, 1, NODES, 128), F32),
        in_specs=specs,
        out_specs=vmem,
        scratch_shapes=scratch,
        compiler_params=pltpu.CompilerParams(
            collective_id=0, has_side_effects=True, vmem_limit_bytes=56 * 2**20
        ),
        cost_estimate=pl.CostEstimate(flops=10**10, bytes_accessed=10**7, transcendentals=10**6),
    )(gl.reshape(GROWS * GCOLS, C), *rest)


def solution(mesh):
    return jax.shard_map(
        per_device,
        mesh=mesh,
        in_specs=(
            P("lat", "lon", None),
            P("lat", "lon", None, None),
            P("lat", "lon", None, None),
            P("lat", "lon", None),
            P("lat", "lon", None),
            P("lat", "lon", None, None),
            P("lat", "lon", None),
            P("lat", "lon", None),
            P(None, None, "hid"),
            P(None, None, "hid"),
            P(None, None, "hid"),
            P(None, "hid"),
            P(None, "hid", None),
            P(),
            P(),
            P(),
        ),
        out_specs=P("lat", "lon", None, "hid"),
        check_vma=False,
    )
```
